128 devices in a mesh: tm: 8 (over y_lo, z), space: 16 (over y_hi, x, core).
Axes of the slice: x: 4, y: 4 (y_hi: 2, y_lo: 2; y = y_hi * 2 + y_lo), z: 4, core: 2. Of those that a mesh axis runs over, the one named last changes fastest.
Arguments:
- probes: bfloat16 [384, 256, 1024], P('tm', 'space'), may hold values from -6 to 6
- local_links: int32 [256, 4], P('space'), may hold values from 0 to 15
- remote_links: int32 [256, 2], P('space'), may hold values from 0 to 31
- shared_blocks: int32 [16, 2], P('space'), may hold values from 0 to 15, as said below
- slab_days: int32 [8], P('tm'), may hold values from 1 to 48, 216 in all
- local_coupling: bfloat16 [256, 4, 64, 64], P('space'), may hold values from -0.3125 to 0.3125
- remote_coupling: bfloat16 [256, 2, 64, 64], P('space'), may hold values from -0.3125 to 0.3125
- block_inverse: bfloat16 [256, 64, 64], P('space'), may hold values from -0.0390625 to 0.0390625
- retention: float32 [384, 16384], P('tm', 'space'), as said below
Outputs:
- variance: float32 [384, 16384], P('tm', 'space')
The draws below stay inside these ranges and needn't reach their ends.
Inputs may be any that keep to these rules, and one draw needn't show every extreme that they name: `shared_blocks`: each group's 2 numbers differ, and each list holds the group's last local block. `retention`: share of a node's state carried from one day to the next.
All inputs are finite; a program needn't handle non-finite values. No bound on the sum of `slab_days` on one device may be relied on, other than what follows from the above.
Results may differ from the reference program's by a relative error of at most 0.0028.
Values may be sent and summed in bfloat16 or wider, within the bound.
A program may use at most 192 MiB of HBM per device.

```python
import math
import jax
import jax.numpy as jnp
import numpy as np
from jax import lax

BS = 64
P_SIZE = 16
KLOC = 4
KREM = 2
BND = 2
DAYS = 48
BLK_DEV = 16
CALENDAR_LENGTH = 384
NBLK = 256
MESH_POINT_COUNT = 16384
N_TM = 8
N_SPACE = 16


def draw_shared_blocks(key, part):
    keys = jax.random.split(key, N_SPACE)

    def single_group(group_key):
        order = jax.random.permutation(group_key, BLK_DEV).astype(jnp.int32)
        topmost = BLK_DEV - 1
        order = jnp.where(order == topmost, order[0], order)
        order = order.at[0].set(topmost)
        return order[:BND]
    return jax.vmap(single_group)(keys).astype(jnp.int32)


def draw_retention(key, part):
    intensity_seed = jax.random.fold_in(key, 11)
    shower_seed = jax.random.fold_in(key, 12)
    multiplier_seed = jax.random.fold_in(key, 13)
    lower_limit = 0.05 / CALENDAR_LENGTH
    upper_limit = 1.0 / 30.0
    shower_intensity = jnp.exp(jax.random.uniform(intensity_seed, (1, MESH_POINT_COUNT), jnp.float32, math.log(lower_limit), math.log(upper_limit)))
    shower_sequence = jax.random.uniform(shower_seed, (CALENDAR_LENGTH, 1), jnp.float32) < 4.0 / CALENDAR_LENGTH
    shower_multiplier = jax.random.uniform(multiplier_seed, (CALENDAR_LENGTH, 1), jnp.float32, 0.5, 0.8)
    return (jnp.exp(-shower_intensity) * jnp.where(shower_sequence, shower_multiplier, 1.0)).astype(jnp.float32)


def plant(values, key, least, high):
    shape = values.shape
    place = [jax.random.randint(jax.random.fold_in(key, axis), (), 0, shape[axis]) for axis in range(len(shape))]
    values = values.at[tuple(place)].set(least)
    longest = shape.index(max(shape))
    place[longest] = (place[longest] + 1) % shape[longest]
    return values.at[tuple(place)].set(high)


def shard_levels(rng, shape, cuts, smallest, top_value):
    loudness, own = 1.0, jax.random.fold_in(rng, 6)
    for axis_at, blocks in cuts:
        draws = jnp.exp(jax.random.uniform(jax.random.fold_in(own, axis_at), (blocks,), jnp.float32, smallest / len(cuts), top_value / len(cuts)))
        loudness = loudness * jnp.repeat(draws, shape[axis_at] // blocks).reshape([-1 if axis == axis_at else 1 for axis in range(len(shape))])
    return loudness


def length_profile(number_of, total, bound, skew):
    loads = [(1 << 20) // math.isqrt(standing ** skew) + 1 for standing in range(2, number_of + 1)]
    spare, counts = total - bound - (number_of - 1), [1] * (number_of - 1)
    while spare > 0:
        free = [i for i in range(number_of - 1) if counts[i] < bound]
        pool, left = sum([loads[i] for i in free]), spare
        for i in free:
            addition = min(bound - counts[i], max(1, left * loads[i] // pool), spare)
            counts[i] = counts[i] + addition
            spare = spare - addition
    return np.array([bound] + counts)


def ragged_sizes(own_key, amount, total, bound, skew):
    if amount == 2:
        one = jax.random.randint(own_key, (), max(1, total - bound), min(bound, total - 1) + 1)
        return jnp.stack([one, total - one])
    sizes = jnp.asarray(length_profile(amount, total, bound, skew), jnp.int32)
    twos = (amount - 1) // 2
    giver, sink = sizes[1:1 + 2 * twos:2], sizes[2:2 + 2 * twos:2]
    slack = jnp.minimum(giver - 1, bound - sink)
    moved = jax.random.randint(jax.random.fold_in(own_key, 1), (twos,), 0, 1 << 20) % (slack + 1)
    sizes = sizes.at[1:1 + 2 * twos:2].set(giver - moved).at[2:2 + 2 * twos:2].set(sink + moved)
    return sizes[jax.random.permutation(jax.random.fold_in(own_key, 2), amount)]


def gaussian(rng, shape, deviation, most, cuts=(), kind=jnp.bfloat16):
    drawn = deviation * jax.random.normal(rng, shape, jnp.float32)
    if cuts:
        drawn = drawn * shard_levels(rng, shape, cuts, -0.22, 0.18)
    return jnp.clip(drawn, -most, most).astype(kind)


def setup_inputs(seed: int = 0) -> dict:
    arg_keys = jax.random.split(jax.random.key(seed), 10)
    return {
        "probes": gaussian(arg_keys[0], (CALENDAR_LENGTH, NBLK, BS * P_SIZE), 1.0, 6.0, ((0, 8), (1, 16))),
        "local_links": plant(jax.random.randint(arg_keys[1], (NBLK, KLOC), 0, BLK_DEV), jax.random.fold_in(arg_keys[1], 1), 0, BLK_DEV - 1).astype(jnp.int32),
        "remote_links": plant(jax.random.randint(arg_keys[2], (NBLK, KREM), 0, N_SPACE * BND), jax.random.fold_in(arg_keys[2], 1), 0, (N_SPACE * BND) - 1).astype(jnp.int32),
        "shared_blocks": draw_shared_blocks(jax.random.fold_in(arg_keys[9], 71), 0),
        "slab_days": ragged_sizes(arg_keys[4], N_TM, DAYS + (N_TM - 1) * (DAYS // 2), DAYS, 2).astype(jnp.int32),
        "local_coupling": gaussian(arg_keys[5], (NBLK, KLOC, BS, BS), (BS * (KLOC + KREM)) ** -0.5, 0.3125, ((0, 16),)),
        "remote_coupling": gaussian(arg_keys[6], (NBLK, KREM, BS, BS), (BS * (KLOC + KREM)) ** -0.5, 0.3125, ((0, 16),)),
        "block_inverse": gaussian(arg_keys[7], (NBLK, BS, BS), (BS * CALENDAR_LENGTH) ** -0.5, 0.0390625, ((0, 16),)),
        "retention": draw_retention(jax.random.fold_in(arg_keys[9], 71), 0),
    }


def reference(probes, local_links, remote_links, shared_blocks, slab_days, local_coupling, remote_coupling, block_inverse, retention):
    shaped = probes.reshape(CALENDAR_LENGTH, NBLK, BS, P_SIZE)
    owners = (jnp.arange(NBLK) // BLK_DEV).astype(jnp.int32)[:, None]
    local_global = owners * BLK_DEV + local_links
    shared_global = (jnp.arange(N_SPACE).astype(jnp.int32)[:, None] * BLK_DEV + shared_blocks).reshape(-1)
    remote_global = shared_global[remote_links]
    day_index = jnp.arange(CALENDAR_LENGTH).astype(jnp.int32)
    active = (day_index % DAYS < slab_days[day_index // DAYS]).astype(jnp.float32)
    retain = jnp.where(active[:, None] > 0, retention, 1.0).reshape(CALENDAR_LENGTH, NBLK, BS, 1)
    local_wide = local_coupling.astype(jnp.float32)
    remote_wide = remote_coupling.astype(jnp.float32)
    inverse_wide = block_inverse.astype(jnp.float32)

    def advance(propagated_vector, argument_bundle):
        present_date, shower_multiplier, marked_entries = argument_bundle
        wide = present_date.astype(jnp.float32)
        running = wide
        for column in range(KLOC):
            running = running - jnp.einsum("bij,bjp->bip", local_wide[:, column], wide[local_global[:, column]])
        for column in range(KREM):
            running = running - jnp.einsum("bij,bjp->bip", remote_wide[:, column], wide[remote_global[:, column]])
        source = running.astype(jnp.bfloat16)
        driving_source = jnp.einsum("bij,bjp->bip", inverse_wide, source.astype(jnp.float32)) * marked_entries
        propagated_vector = shower_multiplier * propagated_vector + driving_source
        return propagated_vector, propagated_vector.astype(jnp.bfloat16)

    start = jnp.zeros((NBLK, BS, P_SIZE), jnp.float32)
    unused, stored = lax.scan(advance, start, (shaped, retain, active))

    def retreat(propagated_vector, argument_bundle):
        saved_calendar_index, present_date, shower_multiplier, marked_entries = argument_bundle
        adjoint = jnp.einsum("bji,bjp->bip", inverse_wide, saved_calendar_index.astype(jnp.float32)) * marked_entries
        present_vector = adjoint + propagated_vector
        approximation = jnp.mean(present_date.astype(jnp.float32) * present_vector, axis=-1).reshape(-1)
        return shower_multiplier * present_vector, approximation

    unused_back, variance = lax.scan(retreat, start, (stored, shaped, retain, active), reverse=True)
    return variance
```

```python
import functools

import jax
import jax.numpy as jnp
from jax import lax
from jax.experimental import pallas as pl
from jax.experimental.pallas import tpu as pltpu
from jax.sharding import PartitionSpec as P

F32, BF16 = jnp.float32, jnp.bfloat16
MESH = pl.DeviceIdType.MESH
DAYS, BLOCKS, BS, PROBES, GROUPS, SLABS = 48, 16, 64, 16, 16, 8
WIDTH = BLOCKS * BS
ROWS = DAYS * PROBES
CHUNKS = 2
CHUNK_ROWS = ROWS // CHUNKS
CHUNK_DAYS = DAYS // CHUNKS
HALF = CHUNK_ROWS // 2
SUB = 192


def day_rows(t):
    return pl.ds(pl.multiple_of(t * PROBES, PROBES), PROBES)


def kernel(
    local_links,
    remote_links,
    shared_blocks,
    slab_days,
    probes_hbm,
    local_hbm,
    remote_hbm,
    inverse_hbm,
    retention_ref,
    out_ref,
    probes,
    local_w,
    remote_w,
    inverse_w,
    shuffle,
    shuffled,
    ordered,
    shared,
    near,
    far,
    forth,
    back,
    total,
    states,
    stored,
    retain,
    active,
    forward_decay,
    backward_decay,
    partial,
    slab_decay,
    ends,
    leaving,
    in_sem,
    send_sem,
    recv_sem,
    tm_send,
    tm_recv,
):
    tm = lax.axis_index("tm")
    space = lax.axis_index("space")
    core, x, y = space % 2, (space // 2) % 4, space // 8

    def at(dx, dy, dc):
        return ((y + dy) % 2 * 4 + (x + dx) % 4) * 2 + (core + dc) % 2

    me = at(0, 0, 0)
    sibling = at(0, 0, 1)

    barrier = pltpu.get_barrier_semaphore()
    for to in (at(1, 0, 0), at(3, 0, 0), at(0, 1, 0), sibling):
        pl.semaphore_signal(barrier, inc=1, device_id=(tm, to), device_id_type=MESH)
    for d in range(1, SLABS):
        pl.semaphore_signal(
            barrier, inc=1, device_id=((tm + d) % SLABS, space), device_id_type=MESH
        )

    fetch = []
    for k in range(CHUNKS):
        rows = pl.ds(k * CHUNK_ROWS, CHUNK_ROWS)
        fetch.append(pltpu.make_async_copy(probes_hbm.at[rows], probes.at[rows], in_sem.at[k]))
    weights = [
        pltpu.make_async_copy(local_hbm, local_w, in_sem.at[CHUNKS]),
        pltpu.make_async_copy(remote_hbm, remote_w, in_sem.at[CHUNKS + 1]),
        pltpu.make_async_copy(inverse_hbm, inverse_w, in_sem.at[CHUNKS + 2]),
    ]
    for copy in fetch + weights:
        copy.start()

    def shuffle_rows(r, carry):
        source = lax.broadcasted_iota(jnp.int32, (64, WIDTH), 0) + r * 64
        target = lax.broadcasted_iota(jnp.int32, (64, WIDTH), 1)
        hit = target == (source % PROBES) * BS + source // PROBES
        shuffle[pl.ds(pl.multiple_of(r * 64, 64), 64), :] = jnp.where(hit, 1.0, 0.0).astype(BF16)
        return carry

    lax.fori_loop(0, WIDTH // 64, shuffle_rows, 0)

    low = lax.broadcasted_iota(jnp.int32, (8, 128), 1) < BS

    def pair_up(first, second):
        mixed = pltpu.roll(jnp.where(low, second, first), BS, 1)
        return jnp.concatenate(
            [jnp.where(low, first, mixed), jnp.where(low, mixed, second)], axis=0
        ).astype(BF16)

    def block_row(t, b):
        return shuffled[pl.ds(pl.multiple_of((t * BLOCKS + b) * 8, 8), 8), :]

    def permute(k):
        def part(r, carry):
            lo = k * CHUNK_ROWS + r * SUB
            for n in range(4):
                value = jnp.dot(
                    probes[pl.ds(pl.multiple_of(lo, SUB), SUB), :],
                    shuffle[:, n * 256 : (n + 1) * 256],
                    preferred_element_type=F32,
                )
                for h in range(2):
                    shuffled[pl.ds(lo * 8 + 2 * n + h, SUB, stride=8), :] = value[
                        :, h * 128 : (h + 1) * 128
                    ]
            return carry

        lax.fori_loop(0, CHUNK_ROWS // SUB, part, 0)

    def pick_shared(k):
        b0, b1 = shared_blocks[0, 0], shared_blocks[0, 1]

        def day(t, carry):
            first = second = block_row(t + k * CHUNK_DAYS, 0)
            for b in range(1, BLOCKS):
                tile = block_row(t + k * CHUNK_DAYS, b)
                first = jnp.where(b0 == b, tile, first)
                second = jnp.where(b1 == b, tile, second)
            shared[k, me, day_rows(t), :] = pair_up(first, second)
            return carry

        lax.fori_loop(0, CHUNK_DAYS, day, 0)

    def order(k):
        def day(t, carry):
            for pair in range(BLOCKS // 2):
                ordered[day_rows(t), pair * 128 : (pair + 1) * 128] = pair_up(
                    block_row(t, 2 * pair), block_row(t, 2 * pair + 1)
                )
            return carry

        lax.fori_loop(k * CHUNK_DAYS, (k + 1) * CHUNK_DAYS, day, 0)

    used = [0]
    pending = []

    def send(slot, k, lo, rows, to):
        i = used[0]
        used[0] += 1
        where = shared.at[k, slot, pl.ds(lo, rows)]
        copy = pltpu.make_async_remote_copy(
            src_ref=where,
            dst_ref=where,
            send_sem=send_sem.at[i],
            recv_sem=recv_sem.at[i],
            device_id=(tm, to),
            device_id_type=MESH,
        )
        copy.start()
        pending.append(copy)
        return copy

    flows = [{} for _ in range(CHUNKS)]
    across = [[] for _ in range(CHUNKS)]
    N = CHUNK_ROWS

    def send_own(k):
        f = flows[k]
        f["y"] = send(me, k, 0, N, at(0, 1, 0))
        f["p0"] = send(me, k, 0, N, at(1, 0, 0))
        f["m0"] = send(me, k, 0, N, at(3, 0, 0))
        across[k].append(send(me, k, 0, N, sibling))

    def relay_first(k):
        f = flows[k]
        f["y"].wait_recv()
        f["p1"] = send(at(0, 1, 0), k, 0, N, at(1, 0, 0))
        f["m1"] = send(at(0, 1, 0), k, 0, N, at(3, 0, 0))
        across[k].append(send(at(0, 1, 0), k, 0, N, sibling))
        f["p0"].wait_recv()
        f["pp0"] = send(at(3, 0, 0), k, 0, HALF, at(1, 0, 0))
        across[k].append(send(at(3, 0, 0), k, 0, N, sibling))
        f["m0"].wait_recv()
        f["mm0"] = send(at(1, 0, 0), k, HALF, HALF, at(3, 0, 0))
        across[k].append(send(at(1, 0, 0), k, 0, N, sibling))

    def relay_second(k):
        f = flows[k]
        f["p1"].wait_recv()
        f["pp1"] = send(at(3, 1, 0), k, 0, HALF, at(1, 0, 0))
        across[k].append(send(at(3, 1, 0), k, 0, N, sibling))
        f["m1"].wait_recv()
        f["mm1"] = send(at(1, 1, 0), k, HALF, HALF, at(3, 0, 0))
        across[k].append(send(at(1, 1, 0), k, 0, N, sibling))

    def relay_third(k):
        f = flows[k]
        f["pp0"].wait_recv()
        f["mm0"].wait_recv()
        across[k].append(send(at(2, 0, 0), k, 0, N, sibling))
        f["pp1"].wait_recv()
        f["mm1"].wait_recv()
        across[k].append(send(at(2, 1, 0), k, 0, N, sibling))

    def all_here(k):
        for copy in across[k]:
            copy.wait_recv()

    def build(weight, links, count, degree, out):
        def pair_of(pair, carry):
            tiles = [
                jnp.transpose(
                    jnp.concatenate(
                        [weight[2 * pair, n].astype(F32), weight[2 * pair + 1, n].astype(F32)], axis=0
                    )
                )
                for n in range(degree)
            ]
            wanted = [
                jnp.where(low[0:1], links[2 * pair, n], links[2 * pair + 1, n])
                for n in range(degree)
            ]

            def source_block(r, c):
                value = tiles[0] * jnp.where(wanted[0] == r, 1.0, 0.0)
                for n in range(1, degree):
                    value = value + tiles[n] * jnp.where(wanted[n] == r, 1.0, 0.0)
                out[
                    pl.ds(pl.multiple_of(r * BS, BS), BS),
                    pl.ds(pl.multiple_of(pair * 128, 128), 128),
                ] = value.astype(BF16)
                return c

            return lax.fori_loop(0, count, source_block, carry)

        lax.fori_loop(0, BLOCKS // 2, pair_of, 0)

    def build_inverse():
        forth[...] = jnp.zeros_like(forth)
        back[...] = jnp.zeros_like(back)
        gap = jnp.zeros((BS, BS), F32)
        for b in range(BLOCKS):
            quad, place = b // 4, b % 4
            value = inverse_w[b].astype(F32)
            for out, tile in ((forth, jnp.transpose(value)), (back, value)):
                wide = jnp.concatenate([tile, gap] if place % 2 == 0 else [gap, tile], axis=1)
                lane = place // 2 * 128
                out[quad, place * BS : (place + 1) * BS, lane : lane + 128] = wide.astype(BF16)

    def couple_local(k):
        def part(r, carry):
            rows = pl.ds(pl.multiple_of(k * CHUNK_ROWS + r * SUB, SUB), SUB)
            for n in range(4):
                cols = slice(n * 256, (n + 1) * 256)
                total[rows, cols] = ordered[rows, cols].astype(F32) - jnp.dot(
                    ordered[rows, :], near[:, cols], preferred_element_type=F32
                )
            return carry

        lax.fori_loop(0, CHUNK_ROWS // SUB, part, 0)

    def couple_remote(k):
        def part(r, carry):
            rows = pl.ds(pl.multiple_of(k * CHUNK_ROWS + r * SUB, SUB), SUB)
            inner = pl.ds(pl.multiple_of(r * SUB, SUB), SUB)
            left = jnp.concatenate([shared[k, g, inner, :] for g in range(GROUPS)], axis=1)
            for n in range(4):
                cols = slice(n * 256, (n + 1) * 256)
                source = (
                    total[rows, cols] - jnp.dot(left, far[:, cols], preferred_element_type=F32)
                ).astype(BF16)
                states[rows, cols] = jnp.dot(source, forth[n], preferred_element_type=F32)
            return carry

        lax.fori_loop(0, CHUNK_ROWS // SUB, part, 0)

    def scan_forward(k, state):
        def day(t, s):
            s = s * retain[pl.ds(t, 1), :] + states[day_rows(t), :] * active[pl.ds(t, 1), :]
            states[day_rows(t), :] = s
            return s

        return lax.fori_loop(k * CHUNK_DAYS, (k + 1) * CHUNK_DAYS, day, state)

    def prepare_decay():
        on = lax.broadcasted_iota(jnp.int32, (DAYS, WIDTH), 0) < slab_days[0]
        active[...] = jnp.where(on, 1.0, 0.0)
        retain[0:DAYS, :] = jnp.where(on, retention_ref[...], 1.0)
        retain[DAYS : DAYS + 8, :] = jnp.ones((8, WIDTH), F32)

        def ahead(t, d):
            d = d * retain[pl.ds(t, 1), :]
            forward_decay[pl.ds(t, 1), :] = d
            return d

        product = lax.fori_loop(0, DAYS, ahead, jnp.ones((1, WIDTH), F32))

        def behind(i, d):
            t = DAYS - 1 - i
            d = d * retain[pl.ds(t + 1, 1), :]
            backward_decay[pl.ds(t, 1), :] = d
            return d

        lax.fori_loop(0, DAYS, behind, jnp.ones((1, WIDTH), F32))
        for q in range(8):
            slab_decay[tm, q : q + 1, :] = product[:, q * 128 : (q + 1) * 128]

    def tm_copy(buf, kind, d):
        to = (tm + d) % SLABS if kind < 2 else (tm + SLABS - d) % SLABS
        return pltpu.make_async_remote_copy(
            src_ref=buf.at[tm],
            dst_ref=buf.at[tm],
            send_sem=tm_send.at[kind * 8 + d],
            recv_sem=tm_recv.at[kind * 8 + d],
            device_id=(to, space),
            device_id_type=MESH,
        )

    def decay_of(s):
        return jnp.concatenate([slab_decay[s, q : q + 1, :] for q in range(8)], axis=1)

    for k in range(CHUNKS):
        fetch[k].wait()
        permute(k)
        pick_shared(k)
    pl.semaphore_wait(barrier, 4 + SLABS - 1)
    for k in range(CHUNKS):
        send_own(k)
    prepare_decay()
    decay_copies = [tm_copy(slab_decay, 0, d) for d in range(1, SLABS)]
    for copy in decay_copies:
        copy.start()
    order(0)
    relay_first(0)
    order(1)
    relay_first(1)
    weights[0].wait()
    build(local_w, local_links, BLOCKS, 4, near)
    relay_second(0)
    weights[1].wait()
    build(remote_w, remote_links, 2 * GROUPS, 2, far)
    relay_second(1)
    couple_local(0)
    relay_third(0)
    couple_local(1)
    weights[2].wait()
    build_inverse()
    all_here(0)
    couple_remote(0)
    state = scan_forward(0, jnp.zeros((PROBES, WIDTH), F32))
    relay_third(1)
    all_here(1)
    couple_remote(1)
    state = scan_forward(1, state)
    ends[tm] = state
    for d in range(1, SLABS):

        @pl.when(tm + d < SLABS)
        def _():
            tm_copy(ends, 1, d).start()

    for copy in decay_copies:
        copy.wait_recv()
    for d in range(1, SLABS):

        @pl.when(tm - d >= 0)
        def _():
            tm_copy(ends, 1, d).wait_recv()

    carry = jnp.zeros((PROBES, WIDTH), F32)
    for s in range(SLABS - 1):
        carry = jnp.where(s < tm, decay_of(s) * carry + ends[s], carry)

    leave = jnp.zeros((PROBES, WIDTH), F32)
    for k in reversed(range(CHUNKS)):

        def fix(t, c):
            stored[day_rows(t), :] = (
                states[day_rows(t), :] + forward_decay[pl.ds(t, 1), :] * c
            ).astype(BF16)
            return c

        carry = lax.fori_loop(k * CHUNK_DAYS, (k + 1) * CHUNK_DAYS, fix, carry)

        def part(r, c):
            rows = pl.ds(pl.multiple_of(k * CHUNK_ROWS + r * SUB, SUB), SUB)
            for n in range(4):
                cols = slice(n * 256, (n + 1) * 256)
                total[rows, cols] = jnp.dot(stored[rows, cols], back[n], preferred_element_type=F32)
            return c

        lax.fori_loop(0, CHUNK_ROWS // SUB, part, 0)

        def day(i, u):
            t = (k + 1) * CHUNK_DAYS - 1 - i
            u = total[day_rows(t), :] * active[pl.ds(t, 1), :] + retain[pl.ds(t + 1, 1), :] * u
            partial[pl.ds(t, 1), :] = jnp.sum(
                ordered[day_rows(t), :].astype(F32) * u, axis=0, keepdims=True
            )
            return u

        leave = lax.fori_loop(0, CHUNK_DAYS, day, leave)
    leaving[tm] = leave * retain[0:1, :]
    for d in range(1, SLABS):

        @pl.when(tm - d >= 0)
        def _():
            tm_copy(leaving, 2, d).start()

    for copy in pending:
        copy.wait_send()
    for copy in decay_copies:
        copy.wait_send()
    for d in range(1, SLABS):

        @pl.when(tm + d < SLABS)
        def _():
            tm_copy(ends, 1, d).wait_send()
            tm_copy(leaving, 2, d).wait_recv()

    carry = jnp.zeros((PROBES, WIDTH), F32)
    for s in reversed(range(1, SLABS)):
        carry = jnp.where(s > tm, decay_of(s) * carry + leaving[s], carry)

    def finish(t, c):
        extra = jnp.sum(ordered[day_rows(t), :].astype(F32) * c, axis=0, keepdims=True)
        out_ref[pl.ds(t, 1), :] = (
            partial[pl.ds(t, 1), :] + backward_decay[pl.ds(t, 1), :] * extra
        ) * (1.0 / PROBES)
        return c

    lax.fori_loop(0, DAYS, finish, carry)
    for d in range(1, SLABS):

        @pl.when(tm - d >= 0)
        def _():
            tm_copy(leaving, 2, d).wait_send()


def local(
    probes,
    local_links,
    remote_links,
    shared_blocks,
    slab_days,
    local_coupling,
    remote_coupling,
    block_inverse,
    retention,
):
    smem = pl.BlockSpec(memory_space=pltpu.SMEM)
    vmem = pl.BlockSpec(memory_space=pltpu.VMEM)
    anywhere = pl.BlockSpec(memory_space=pl.ANY)
    return pl.pallas_call(
        kernel,
        out_shape=jax.ShapeDtypeStruct((DAYS, WIDTH), F32),
        in_specs=[smem] * 4 + [anywhere] * 4 + [vmem],
        out_specs=vmem,
        scratch_shapes=[
            pltpu.VMEM((ROWS, WIDTH), BF16),
            pltpu.VMEM(local_coupling.shape, BF16),
            pltpu.VMEM(remote_coupling.shape, BF16),
            pltpu.VMEM(block_inverse.shape, BF16),
            pltpu.VMEM((WIDTH, WIDTH), BF16),
            pltpu.VMEM((ROWS * 8, 128), F32),
            pltpu.VMEM((ROWS, WIDTH), BF16),
            pltpu.VMEM((CHUNKS, GROUPS, CHUNK_ROWS, 128), BF16),
            pltpu.VMEM((WIDTH, WIDTH), BF16),
            pltpu.VMEM((2 * WIDTH, WIDTH), BF16),
            pltpu.VMEM((4, 256, 256), BF16),
            pltpu.VMEM((4, 256, 256), BF16),
            pltpu.VMEM((ROWS, WIDTH), F32),
            pltpu.VMEM((ROWS, WIDTH), F32),
            pltpu.VMEM((ROWS, WIDTH), BF16),
            pltpu.VMEM((DAYS + 8, WIDTH), F32),
            pltpu.VMEM((DAYS, WIDTH), F32),
            pltpu.VMEM((DAYS, WIDTH), F32),
            pltpu.VMEM((DAYS, WIDTH), F32),
            pltpu.VMEM((DAYS, WIDTH), F32),
            pltpu.VMEM((SLABS, 8, 128), F32),
            pltpu.VMEM((SLABS, PROBES, WIDTH), F32),
            pltpu.VMEM((SLABS, PROBES, WIDTH), F32),
            pltpu.SemaphoreType.DMA((CHUNKS + 3,)),
            pltpu.SemaphoreType.DMA((CHUNKS * 20,)),
            pltpu.SemaphoreType.DMA((CHUNKS * 20,)),
            pltpu.SemaphoreType.DMA((24,)),
            pltpu.SemaphoreType.DMA((24,)),
        ],
        compiler_params=pltpu.CompilerParams(
            vmem_limit_bytes=60 << 20, collective_id=0, has_side_effects=True
        ),
    )(
        local_links,
        remote_links,
        shared_blocks,
        slab_days,
        probes.reshape(ROWS, WIDTH),
        local_coupling,
        remote_coupling,
        block_inverse,
        retention,
    )


def solution(mesh):
    placed = (
        P("tm", "space", None),
        P("space", None),
        P("space", None),
        P("space", None),
        P("tm"),
        P("space", None, None, None),
        P("space", None, None, None),
        P("space", None, None),
        P("tm", "space"),
    )
    return jax.shard_map(
        local, mesh=mesh, in_specs=placed, out_specs=P("tm", "space"), check_vma=False
    )
```

```python
import functools

import jax
import jax.numpy as jnp
from jax import lax
from jax.experimental import pallas as pl
from jax.experimental.pallas import tpu as pltpu
from jax.sharding import PartitionSpec as P

F32, BF16 = jnp.float32, jnp.bfloat16
MESH = pl.DeviceIdType.MESH
DAYS, BLOCKS, BS, PROBES, GROUPS, SLABS = 48, 16, 64, 16, 16, 8
WIDTH = BLOCKS * BS
ROWS = DAYS * PROBES
CHUNKS = 2
CHUNK_ROWS = ROWS // CHUNKS
CHUNK_DAYS = DAYS // CHUNKS
HALF = CHUNK_ROWS // 2
SUB = 192


def day_rows(t):
    return pl.ds(pl.multiple_of(t * PROBES, PROBES), PROBES)


def kernel(
    local_links,
    remote_links,
    shared_blocks,
    slab_days,
    probes_hbm,
    local_hbm,
    remote_hbm,
    inverse_hbm,
    retention_ref,
    out_ref,
    probes,
    local_w,
    remote_w,
    inverse_w,
    shuffle,
    shuffled,
    picked,
    picked_shuffled,
    ordered,
    shared,
    tiles,
    near,
    far,
    forth,
    back,
    total,
    states,
    stored,
    retain,
    active,
    forward_decay,
    backward_decay,
    partial,
    slab_decay,
    ends,
    leaving,
    in_sem,
    send_sem,
    recv_sem,
    tm_send,
    tm_recv,
):
    tm = lax.axis_index("tm")
    space = lax.axis_index("space")
    core, x, y = space % 2, (space // 2) % 4, space // 8

    def at(dx, dy, dc):
        return ((y + dy) % 2 * 4 + (x + dx) % 4) * 2 + (core + dc) % 2

    me = at(0, 0, 0)
    sibling = at(0, 0, 1)

    barrier = pltpu.get_barrier_semaphore()
    for to in (at(1, 0, 0), at(3, 0, 0), at(0, 1, 0), sibling):
        pl.semaphore_signal(barrier, inc=1, device_id=(tm, to), device_id_type=MESH)
    for d in range(1, SLABS):
        pl.semaphore_signal(
            barrier, inc=1, device_id=((tm + d) % SLABS, space), device_id_type=MESH
        )

    fetch = []
    for k in range(CHUNKS):
        rows = pl.ds(k * CHUNK_ROWS, CHUNK_ROWS)
        fetch.append(pltpu.make_async_copy(probes_hbm.at[rows], probes.at[rows], in_sem.at[k]))
    weights = [
        pltpu.make_async_copy(local_hbm, local_w, in_sem.at[CHUNKS]),
        pltpu.make_async_copy(remote_hbm, remote_w, in_sem.at[CHUNKS + 1]),
        pltpu.make_async_copy(inverse_hbm, inverse_w, in_sem.at[CHUNKS + 2]),
    ]
    for copy in fetch + weights:
        copy.start()

    def shuffle_rows(r, carry):
        source = lax.broadcasted_iota(jnp.int32, (64, WIDTH), 0) + r * 64
        target = lax.broadcasted_iota(jnp.int32, (64, WIDTH), 1)
        hit = target == (source % PROBES) * BS + source // PROBES
        shuffle[pl.ds(pl.multiple_of(r * 64, 64), 64), :] = jnp.where(hit, 1.0, 0.0).astype(BF16)
        return carry

    lax.fori_loop(0, WIDTH // 64, shuffle_rows, 0)

    low = lax.broadcasted_iota(jnp.int32, (8, 128), 1) < BS

    def pair_up(first, second):
        mixed = pltpu.roll(jnp.where(low, second, first), BS, 1)
        return jnp.concatenate(
            [jnp.where(low, first, mixed), jnp.where(low, mixed, second)], axis=0
        )

    def block_row(t, b):
        return shuffled[pl.ds(pl.multiple_of((t * BLOCKS + b) * 8, 8), 8), :]

    def permute(k):
        def part(r, carry):
            lo = k * CHUNK_ROWS + r * SUB
            for n in range(4):
                value = jnp.dot(
                    probes[pl.ds(pl.multiple_of(lo, SUB), SUB), :],
                    shuffle[:, n * 256 : (n + 1) * 256],
                    preferred_element_type=F32,
                )
                for h in range(2):
                    shuffled[pl.ds(lo * 8 + 2 * n + h, SUB, stride=8), :] = value[
                        :, h * 128 : (h + 1) * 128
                    ]
            return carry

        lax.fori_loop(0, CHUNK_ROWS // SUB, part, 0)

    def pick_shared():
        row = lax.broadcasted_iota(jnp.int32, (2 * DAYS, ROWS), 0)
        column = lax.broadcasted_iota(jnp.int32, (2 * DAYS, ROWS), 1)
        second = row >= DAYS
        day = jnp.where(second, row - DAYS, row)
        wanted = day * BLOCKS + jnp.where(second, shared_blocks[0, 1], shared_blocks[0, 0])
        select = jnp.where(column == wanted, 1.0, 0.0).astype(BF16)
        for n in range(4):
            cols = slice(n * 256, (n + 1) * 256)
            picked[:, cols] = jnp.dot(
                select, probes[:, cols], preferred_element_type=F32
            ).astype(BF16)
        for n in range(4):
            value = jnp.dot(
                picked[...], shuffle[:, n * 256 : (n + 1) * 256], preferred_element_type=F32
            )
            for h in range(2):
                picked_shuffled[pl.ds(2 * n + h, 2 * DAYS, stride=8), :] = value[
                    :, h * 128 : (h + 1) * 128
                ]

        def days(g, carry):
            for i in range(4):
                t = g * 4 + i
                tiles = [
                    picked_shuffled[pl.ds(pl.multiple_of((m * DAYS + t) * 8, 8), 8), :]
                    for m in range(2)
                ]
                shared[t // CHUNK_DAYS, me, day_rows(t % CHUNK_DAYS), :] = pair_up(*tiles).astype(BF16)
            return carry

        lax.fori_loop(0, DAYS // 4, days, 0)

    def order(k):
        def days(g, carry):
            for i in range(4):
                t = g * 4 + i
                for pair in range(BLOCKS // 2):
                    value = pair_up(block_row(t, 2 * pair), block_row(t, 2 * pair + 1))
                    total[day_rows(t), pair * 128 : (pair + 1) * 128] = value
                    ordered[day_rows(t), pair * 128 : (pair + 1) * 128] = value.astype(BF16)
            return carry

        lax.fori_loop(k * CHUNK_DAYS // 4, (k + 1) * CHUNK_DAYS // 4, days, 0)

    used = [0]
    pending = []

    def send(slot, k, lo, rows, to):
        i = used[0]
        used[0] += 1
        where = shared.at[k, slot, pl.ds(lo, rows)]
        copy = pltpu.make_async_remote_copy(
            src_ref=where,
            dst_ref=where,
            send_sem=send_sem.at[i],
            recv_sem=recv_sem.at[i],
            device_id=(tm, to),
            device_id_type=MESH,
        )
        copy.start()
        pending.append(copy)
        return copy

    flows = [{} for _ in range(CHUNKS)]
    across = [[] for _ in range(CHUNKS)]
    N = CHUNK_ROWS

    def send_own(k):
        f = flows[k]
        f["y"] = send(me, k, 0, N, at(0, 1, 0))
        f["p0"] = send(me, k, 0, N, at(1, 0, 0))
        f["m0"] = send(me, k, 0, N, at(3, 0, 0))
        across[k].append(send(me, k, 0, N, sibling))

    def relay_first(k):
        f = flows[k]
        f["y"].wait_recv()
        f["p1"] = send(at(0, 1, 0), k, 0, N, at(1, 0, 0))
        f["m1"] = send(at(0, 1, 0), k, 0, N, at(3, 0, 0))
        across[k].append(send(at(0, 1, 0), k, 0, N, sibling))
        f["p0"].wait_recv()
        f["pp0"] = send(at(3, 0, 0), k, 0, HALF, at(1, 0, 0))
        across[k].append(send(at(3, 0, 0), k, 0, N, sibling))
        f["m0"].wait_recv()
        f["mm0"] = send(at(1, 0, 0), k, HALF, HALF, at(3, 0, 0))
        across[k].append(send(at(1, 0, 0), k, 0, N, sibling))

    def relay_second(k):
        f = flows[k]
        f["p1"].wait_recv()
        f["pp1"] = send(at(3, 1, 0), k, 0, HALF, at(1, 0, 0))
        across[k].append(send(at(3, 1, 0), k, 0, N, sibling))
        f["m1"].wait_recv()
        f["mm1"] = send(at(1, 1, 0), k, HALF, HALF, at(3, 0, 0))
        across[k].append(send(at(1, 1, 0), k, 0, N, sibling))

    def relay_third(k):
        f = flows[k]
        f["pp0"].wait_recv()
        f["mm0"].wait_recv()
        across[k].append(send(at(2, 0, 0), k, 0, N, sibling))
        f["pp1"].wait_recv()
        f["mm1"].wait_recv()
        across[k].append(send(at(2, 1, 0), k, 0, N, sibling))

    def all_here(k):
        for copy in across[k]:
            copy.wait_recv()

    def turn(weight, degree, first):
        for pair in range(BLOCKS // 2):
            for n in range(degree):
                tiles[pair, first + n] = jnp.transpose(
                    jnp.concatenate(
                        [weight[2 * pair, n].astype(F32), weight[2 * pair + 1, n].astype(F32)], axis=0
                    )
                ).astype(BF16)

    def build(links, count, degree, first, out):
        def pair_of(pair, carry):
            parts = [tiles[pair, first + n] for n in range(degree)]
            wanted = [
                jnp.where(low[0:1], links[n, 2 * pair], links[n, 2 * pair + 1])
                for n in range(degree)
            ]

            def source_blocks(g, c):
                for i in range(4):
                    r = g * 4 + i
                    terms = [
                        p * jnp.where(w == r, 1.0, 0.0).astype(BF16) for p, w in zip(parts, wanted)
                    ]
                    out[
                        pl.ds(pl.multiple_of(r * BS, BS), BS),
                        pl.ds(pl.multiple_of(pair * 128, 128), 128),
                    ] = functools.reduce(lambda u, v: u + v, terms)
                return c

            return lax.fori_loop(0, count // 4, source_blocks, carry)

        lax.fori_loop(0, BLOCKS // 2, pair_of, 0)

    def build_inverse():
        forth[...] = jnp.zeros_like(forth)
        back[...] = jnp.zeros_like(back)
        gap = jnp.zeros((BS, BS), F32)
        for b in range(BLOCKS):
            quad, place = b // 4, b % 4
            value = inverse_w[b].astype(F32)
            for out, tile in ((forth, jnp.transpose(value)), (back, value)):
                wide = jnp.concatenate([tile, gap] if place % 2 == 0 else [gap, tile], axis=1)
                lane = place // 2 * 128
                out[quad, place * BS : (place + 1) * BS, lane : lane + 128] = wide.astype(BF16)

    def couple_local(k):
        def part(r, carry):
            rows = pl.ds(pl.multiple_of(k * CHUNK_ROWS + r * SUB, SUB), SUB)
            for n in range(4):
                cols = slice(n * 256, (n + 1) * 256)
                total[rows, cols] = total[rows, cols] - jnp.dot(
                    ordered[rows, :], near[:, cols], preferred_element_type=F32
                )
            return carry

        lax.fori_loop(0, CHUNK_ROWS // SUB, part, 0)

    def couple_remote(k):
        def part(r, carry):
            rows = pl.ds(pl.multiple_of(k * CHUNK_ROWS + r * SUB, SUB), SUB)
            inner = pl.ds(pl.multiple_of(r * SUB, SUB), SUB)
            for n in range(4):
                cols = slice(n * 256, (n + 1) * 256)
                left = jnp.concatenate([shared[k, g, inner, :] for g in range(GROUPS)], axis=1)
                total[rows, cols] = total[rows, cols] - jnp.dot(
                    left, far[:, cols], preferred_element_type=F32
                )
            for n in range(4):
                cols = slice(n * 256, (n + 1) * 256)
                states[rows, cols] = jnp.dot(
                    total[rows, cols].astype(BF16), forth[n], preferred_element_type=F32
                )
            return carry

        lax.fori_loop(0, CHUNK_ROWS // SUB, part, 0)

    def scan_forward(k, state):
        def day(t, s):
            s = s * retain[pl.ds(t, 1), :] + states[day_rows(t), :] * active[pl.ds(t, 1), :]
            states[day_rows(t), :] = s
            return s

        return lax.fori_loop(k * CHUNK_DAYS, (k + 1) * CHUNK_DAYS, day, state)

    def prepare_decay():
        on = lax.broadcasted_iota(jnp.int32, (DAYS, WIDTH), 0) < slab_days[0]
        active[...] = jnp.where(on, 1.0, 0.0)
        retain[0:DAYS, :] = jnp.where(on, retention_ref[...], 1.0)
        retain[DAYS : DAYS + 8, :] = jnp.ones((8, WIDTH), F32)

        def ahead(t, d):
            d = d * retain[pl.ds(t, 1), :]
            forward_decay[pl.ds(t, 1), :] = d
            return d

        product = lax.fori_loop(0, DAYS, ahead, jnp.ones((1, WIDTH), F32))

        def behind(i, d):
            t = DAYS - 1 - i
            d = d * retain[pl.ds(t + 1, 1), :]
            backward_decay[pl.ds(t, 1), :] = d
            return d

        lax.fori_loop(0, DAYS, behind, jnp.ones((1, WIDTH), F32))
        for q in range(8):
            slab_decay[tm, q : q + 1, :] = product[:, q * 128 : (q + 1) * 128]

    def tm_copy(buf, kind, d):
        to = (tm + d) % SLABS if kind < 2 else (tm + SLABS - d) % SLABS
        return pltpu.make_async_remote_copy(
            src_ref=buf.at[tm],
            dst_ref=buf.at[tm],
            send_sem=tm_send.at[kind * 8 + d],
            recv_sem=tm_recv.at[kind * 8 + d],
            device_id=(to, space),
            device_id_type=MESH,
        )

    def decay_of(s):
        return jnp.concatenate([slab_decay[s, q : q + 1, :] for q in range(8)], axis=1)

    for k in range(CHUNKS):
        fetch[k].wait()
    pick_shared()
    prepare_decay()
    pl.semaphore_wait(barrier, 4 + SLABS - 1)
    for k in range(CHUNKS):
        send_own(k)
    decay_copies = [tm_copy(slab_decay, 0, d) for d in range(1, SLABS)]
    for copy in decay_copies:
        copy.start()
    permute(0)
    permute(1)
    relay_first(0)
    order(0)
    relay_first(1)
    order(1)
    weights[0].wait()
    turn(local_w, 4, 0)
    build(local_links, BLOCKS, 4, 0, near)
    relay_second(0)
    weights[1].wait()
    turn(remote_w, 2, 4)
    build(remote_links, 2 * GROUPS, 2, 4, far)
    relay_second(1)
    couple_local(0)
    relay_third(0)
    couple_local(1)
    weights[2].wait()
    build_inverse()
    all_here(0)
    couple_remote(0)
    state = scan_forward(0, jnp.zeros((PROBES, WIDTH), F32))
    relay_third(1)
    all_here(1)
    couple_remote(1)
    state = scan_forward(1, state)
    ends[tm] = state
    for d in range(1, SLABS):

        @pl.when(tm + d < SLABS)
        def _():
            tm_copy(ends, 1, d).start()

    for copy in decay_copies:
        copy.wait_recv()
    for d in range(1, SLABS):

        @pl.when(tm - d >= 0)
        def _():
            tm_copy(ends, 1, d).wait_recv()

    carry = jnp.zeros((PROBES, WIDTH), F32)
    for s in range(SLABS - 1):
        carry = jnp.where(s < tm, decay_of(s) * carry + ends[s], carry)

    row8 = lax.broadcasted_iota(jnp.int32, (8, 128), 0)

    def fold(values):
        for step in (1, 2, 4):
            keep = (row8 & step) == 0
            values = [
                jnp.where(keep, u, v) + pltpu.roll(jnp.where(keep, v, u), step, 0)
                for u, v in zip(values[0::2], values[1::2])
            ]
        return values[0]

    def adjoint_sweep(carry, with_sums):
        def fix(g, c):
            for i in range(2):
                t = 2 * g + i
                stored[day_rows(t), :] = (
                    states[day_rows(t), :] + forward_decay[pl.ds(t, 1), :] * c
                ).astype(BF16)
            return c

        lax.fori_loop(0, DAYS // 2, fix, carry)

        def part(r, c):
            rows = pl.ds(pl.multiple_of(r * SUB, SUB), SUB)
            for n in range(4):
                cols = slice(n * 256, (n + 1) * 256)
                total[rows, cols] = jnp.dot(stored[rows, cols], back[n], preferred_element_type=F32)
            return c

        lax.fori_loop(0, ROWS // SUB, part, 0)
        leave = []
        for n in range(4):
            cols = slice(n * 256, (n + 1) * 256)

            def days(i, u):
                g = DAYS // 8 - 1 - i
                sums = [[None] * 8, [None] * 8]
                for j in reversed(range(8)):
                    t = g * 8 + j
                    u = total[day_rows(t), cols] * active[pl.ds(t, 1), cols] + retain[
                        pl.ds(t + 1, 1), cols
                    ] * u
                    if with_sums:
                        product = ordered[day_rows(t), cols].astype(F32) * u
                        for h in range(2):
                            half = product[:, h * 128 : (h + 1) * 128]
                            sums[h][j] = half[0:8] + half[8:16]
                if with_sums:
                    eight = pl.ds(pl.multiple_of(g * 8, 8), 8)
                    for h in range(2):
                        lane = n * 256 + h * 128
                        partial[eight, lane : lane + 128] = fold(sums[h])
                return u

            leave.append(
                lax.fori_loop(0, DAYS // 8, days, jnp.zeros((PROBES, 256), F32))
                * retain[0:1, cols]
            )
        return leave

    leave = adjoint_sweep(carry, True)
    for n in range(4):
        leaving[tm, :, n * 256 : (n + 1) * 256] = leave[n]
    for d in range(1, SLABS):

        @pl.when(tm - d >= 0)
        def _():
            tm_copy(leaving, 2, d).start()

    for copy in pending:
        copy.wait_send()
    for copy in decay_copies:
        copy.wait_send()
    for d in range(1, SLABS):

        @pl.when(tm + d < SLABS)
        def _():
            tm_copy(ends, 1, d).wait_send()
            tm_copy(leaving, 2, d).wait_recv()

    carry = jnp.zeros((PROBES, WIDTH), F32)
    for s in reversed(range(1, SLABS)):
        carry = jnp.where(s > tm, decay_of(s) * carry + leaving[s], carry)

    for n in range(8):
        cols = slice(n * 128, (n + 1) * 128)
        part_carry = carry[:, cols]

        def finish(g, c):
            eight = pl.ds(pl.multiple_of(g * 8, 8), 8)
            z = ordered[pl.ds(pl.multiple_of(g * 128, 128), 128), cols].astype(F32)
            extra = fold(
                [
                    z[16 * d : 16 * d + 8] * c[0:8] + z[16 * d + 8 : 16 * d + 16] * c[8:16]
                    for d in range(8)
                ]
            )
            out_ref[eight, cols] = (partial[eight, cols] + backward_decay[eight, cols] * extra) * (
                1.0 / PROBES
            )
            return c

        lax.fori_loop(0, DAYS // 8, finish, part_carry)
    for d in range(1, SLABS):

        @pl.when(tm - d >= 0)
        def _():
            tm_copy(leaving, 2, d).wait_send()


def local(
    probes,
    local_links,
    remote_links,
    shared_blocks,
    slab_days,
    local_coupling,
    remote_coupling,
    block_inverse,
    retention,
):
    smem = pl.BlockSpec(memory_space=pltpu.SMEM)
    vmem = pl.BlockSpec(memory_space=pltpu.VMEM)
    anywhere = pl.BlockSpec(memory_space=pl.ANY)
    return pl.pallas_call(
        kernel,
        out_shape=jax.ShapeDtypeStruct((DAYS, WIDTH), F32),
        in_specs=[smem] * 4 + [anywhere] * 4 + [vmem],
        out_specs=vmem,
        scratch_shapes=[
            pltpu.VMEM((ROWS, WIDTH), BF16),
            pltpu.VMEM(local_coupling.shape, BF16),
            pltpu.VMEM(remote_coupling.shape, BF16),
            pltpu.VMEM(block_inverse.shape, BF16),
            pltpu.VMEM((WIDTH, WIDTH), BF16),
            pltpu.VMEM((ROWS * 8, 128), F32),
            pltpu.VMEM((2 * DAYS, WIDTH), BF16),
            pltpu.VMEM((2 * DAYS * 8, 128), F32),
            pltpu.VMEM((ROWS, WIDTH), BF16),
            pltpu.VMEM((CHUNKS, GROUPS, CHUNK_ROWS, 128), BF16),
            pltpu.VMEM((BLOCKS // 2, 6, BS, 128), BF16),
            pltpu.VMEM((WIDTH, WIDTH), BF16),
            pltpu.VMEM((2 * WIDTH, WIDTH), BF16),
            pltpu.VMEM((4, 256, 256), BF16),
            pltpu.VMEM((4, 256, 256), BF16),
            pltpu.VMEM((ROWS, WIDTH), F32),
            pltpu.VMEM((ROWS, WIDTH), F32),
            pltpu.VMEM((ROWS, WIDTH), BF16),
            pltpu.VMEM((DAYS + 8, WIDTH), F32),
            pltpu.VMEM((DAYS, WIDTH), F32),
            pltpu.VMEM((DAYS, WIDTH), F32),
            pltpu.VMEM((DAYS, WIDTH), F32),
            pltpu.VMEM((DAYS, WIDTH), F32),
            pltpu.VMEM((SLABS, 8, 128), F32),
            pltpu.VMEM((SLABS, PROBES, WIDTH), F32),
            pltpu.VMEM((SLABS, PROBES, WIDTH), F32),
            pltpu.SemaphoreType.DMA((CHUNKS + 3,)),
            pltpu.SemaphoreType.DMA((CHUNKS * 20,)),
            pltpu.SemaphoreType.DMA((CHUNKS * 20,)),
            pltpu.SemaphoreType.DMA((24,)),
            pltpu.SemaphoreType.DMA((24,)),
        ],
        compiler_params=pltpu.CompilerParams(
            vmem_limit_bytes=60 << 20, collective_id=0, has_side_effects=True
        ),
    )(
        local_links.T,
        remote_links.T,
        shared_blocks,
        slab_days,
        probes.reshape(ROWS, WIDTH),
        local_coupling,
        remote_coupling,
        block_inverse,
        retention,
    )


def solution(mesh):
    placed = (
        P("tm", "space", None),
        P("space", None),
        P("space", None),
        P("space", None),
        P("tm"),
        P("space", None, None, None),
        P("space", None, None, None),
        P("space", None, None),
        P("tm", "space"),
    )
    return jax.shard_map(
        local, mesh=mesh, in_specs=placed, out_specs=P("tm", "space"), check_vma=False
    )
```

```python
import functools

import jax
import jax.numpy as jnp
from jax import lax
from jax.experimental import pallas as pl
from jax.experimental.pallas import tpu as pltpu
from jax.sharding import PartitionSpec as P

F32, BF16 = jnp.float32, jnp.bfloat16
MESH = pl.DeviceIdType.MESH
DAYS, BLOCKS, BS, PROBES, GROUPS, SLABS = 48, 16, 64, 16, 16, 8
WIDTH = BLOCKS * BS
ROWS = DAYS * PROBES
CHUNKS = 2
CHUNK_ROWS = ROWS // CHUNKS
CHUNK_DAYS = DAYS // CHUNKS
HALF = CHUNK_ROWS // 2
SUB = 192


def day_rows(t):
    return pl.ds(pl.multiple_of(t * PROBES, PROBES), PROBES)


def kernel(
    local_links,
    remote_links,
    shared_blocks,
    slab_days,
    probes_hbm,
    local_hbm,
    remote_hbm,
    inverse_hbm,
    retention_ref,
    out_ref,
    probes,
    local_w,
    remote_w,
    inverse_w,
    shuffle,
    shuffled,
    picked,
    picked_shuffled,
    ordered,
    shared,
    tiles,
    near,
    far,
    forth,
    back,
    total,
    states,
    stored,
    retain,
    active,
    forward_decay,
    backward_decay,
    partial,
    slab_decay,
    response,
    ends,
    ends_short,
    leaving,
    leaving_short,
    in_sem,
    send_sem,
    recv_sem,
    tm_send,
    tm_recv,
):
    tm = lax.axis_index("tm")
    space = lax.axis_index("space")
    core, x, y = space % 2, (space // 2) % 4, space // 8

    def at(dx, dy, dc):
        return ((y + dy) % 2 * 4 + (x + dx) % 4) * 2 + (core + dc) % 2

    me = at(0, 0, 0)
    sibling = at(0, 0, 1)

    barrier = pltpu.get_barrier_semaphore()
    for to in (at(1, 0, 0), at(3, 0, 0), at(0, 1, 0), sibling):
        pl.semaphore_signal(barrier, inc=1, device_id=(tm, to), device_id_type=MESH)
    for d in range(1, SLABS):
        pl.semaphore_signal(
            barrier, inc=1, device_id=((tm + d) % SLABS, space), device_id_type=MESH
        )

    fetch = []
    for k in range(CHUNKS):
        rows = pl.ds(k * CHUNK_ROWS, CHUNK_ROWS)
        fetch.append(pltpu.make_async_copy(probes_hbm.at[rows], probes.at[rows], in_sem.at[k]))
    weights = [
        pltpu.make_async_copy(local_hbm, local_w, in_sem.at[CHUNKS]),
        pltpu.make_async_copy(remote_hbm, remote_w, in_sem.at[CHUNKS + 1]),
        pltpu.make_async_copy(inverse_hbm, inverse_w, in_sem.at[CHUNKS + 2]),
    ]
    for copy in fetch + weights:
        copy.start()

    def shuffle_rows(r, carry):
        source = lax.broadcasted_iota(jnp.int32, (64, WIDTH), 0) + r * 64
        target = lax.broadcasted_iota(jnp.int32, (64, WIDTH), 1)
        hit = target == (source % PROBES) * BS + source // PROBES
        shuffle[pl.ds(pl.multiple_of(r * 64, 64), 64), :] = jnp.where(hit, 1.0, 0.0).astype(BF16)
        return carry

    lax.fori_loop(0, WIDTH // 64, shuffle_rows, 0)

    low = lax.broadcasted_iota(jnp.int32, (8, 128), 1) < BS

    def pair_up(first, second):
        mixed = pltpu.roll(jnp.where(low, second, first), BS, 1)
        return jnp.concatenate(
            [jnp.where(low, first, mixed), jnp.where(low, mixed, second)], axis=0
        )

    def block_row(t, b):
        return shuffled[pl.ds(pl.multiple_of((t * BLOCKS + b) * 8, 8), 8), :]

    def permute(k):
        def part(r, carry):
            lo = k * CHUNK_ROWS + r * SUB
            for n in range(4):
                value = jnp.dot(
                    probes[pl.ds(pl.multiple_of(lo, SUB), SUB), :],
                    shuffle[:, n * 256 : (n + 1) * 256],
                    preferred_element_type=F32,
                )
                for h in range(2):
                    shuffled[pl.ds(lo * 8 + 2 * n + h, SUB, stride=8), :] = value[
                        :, h * 128 : (h + 1) * 128
                    ]
            return carry

        lax.fori_loop(0, CHUNK_ROWS // SUB, part, 0)

    def pick_shared():
        row = lax.broadcasted_iota(jnp.int32, (2 * DAYS, ROWS), 0)
        column = lax.broadcasted_iota(jnp.int32, (2 * DAYS, ROWS), 1)
        second = row >= DAYS
        day = jnp.where(second, row - DAYS, row)
        wanted = day * BLOCKS + jnp.where(second, shared_blocks[0, 1], shared_blocks[0, 0])
        select = jnp.where(column == wanted, 1.0, 0.0).astype(BF16)
        for n in range(4):
            cols = slice(n * 256, (n + 1) * 256)
            picked[:, cols] = jnp.dot(
                select, probes[:, cols], preferred_element_type=F32
            ).astype(BF16)
        for n in range(4):
            value = jnp.dot(
                picked[...], shuffle[:, n * 256 : (n + 1) * 256], preferred_element_type=F32
            )
            for h in range(2):
                picked_shuffled[pl.ds(2 * n + h, 2 * DAYS, stride=8), :] = value[
                    :, h * 128 : (h + 1) * 128
                ]

        def days(g, carry):
            for i in range(4):
                t = g * 4 + i
                tiles = [
                    picked_shuffled[pl.ds(pl.multiple_of((m * DAYS + t) * 8, 8), 8), :]
                    for m in range(2)
                ]
                shared[t // CHUNK_DAYS, me, day_rows(t % CHUNK_DAYS), :] = pair_up(*tiles).astype(BF16)
            return carry

        lax.fori_loop(0, DAYS // 4, days, 0)

    def order(k):
        def days(g, carry):
            for i in range(4):
                t = g * 4 + i
                for pair in range(BLOCKS // 2):
                    value = pair_up(block_row(t, 2 * pair), block_row(t, 2 * pair + 1))
                    total[day_rows(t), pair * 128 : (pair + 1) * 128] = value
                    ordered[day_rows(t), pair * 128 : (pair + 1) * 128] = value.astype(BF16)
            return carry

        lax.fori_loop(k * CHUNK_DAYS // 4, (k + 1) * CHUNK_DAYS // 4, days, 0)

    used = [0]
    pending = []

    def send(slot, k, lo, rows, to):
        i = used[0]
        used[0] += 1
        where = shared.at[k, slot, pl.ds(lo, rows)]
        copy = pltpu.make_async_remote_copy(
            src_ref=where,
            dst_ref=where,
            send_sem=send_sem.at[i],
            recv_sem=recv_sem.at[i],
            device_id=(tm, to),
            device_id_type=MESH,
        )
        copy.start()
        pending.append(copy)
        return copy

    flows = [{} for _ in range(CHUNKS)]
    across = [[] for _ in range(CHUNKS)]
    N = CHUNK_ROWS

    def send_own(k):
        f = flows[k]
        f["y"] = send(me, k, 0, N, at(0, 1, 0))
        f["p0"] = send(me, k, 0, N, at(1, 0, 0))
        f["m0"] = send(me, k, 0, N, at(3, 0, 0))
        across[k].append(send(me, k, 0, N, sibling))

    def relay_first(k):
        f = flows[k]
        f["y"].wait_recv()
        f["p1"] = send(at(0, 1, 0), k, 0, N, at(1, 0, 0))
        f["m1"] = send(at(0, 1, 0), k, 0, N, at(3, 0, 0))
        across[k].append(send(at(0, 1, 0), k, 0, N, sibling))
        f["p0"].wait_recv()
        f["pp0"] = send(at(3, 0, 0), k, 0, HALF, at(1, 0, 0))
        across[k].append(send(at(3, 0, 0), k, 0, N, sibling))
        f["m0"].wait_recv()
        f["mm0"] = send(at(1, 0, 0), k, HALF, HALF, at(3, 0, 0))
        across[k].append(send(at(1, 0, 0), k, 0, N, sibling))

    def relay_second(k):
        f = flows[k]
        f["p1"].wait_recv()
        f["pp1"] = send(at(3, 1, 0), k, 0, HALF, at(1, 0, 0))
        across[k].append(send(at(3, 1, 0), k, 0, N, sibling))
        f["m1"].wait_recv()
        f["mm1"] = send(at(1, 1, 0), k, HALF, HALF, at(3, 0, 0))
        across[k].append(send(at(1, 1, 0), k, 0, N, sibling))

    def relay_third(k):
        f = flows[k]
        f["pp0"].wait_recv()
        f["mm0"].wait_recv()
        across[k].append(send(at(2, 0, 0), k, 0, N, sibling))
        f["pp1"].wait_recv()
        f["mm1"].wait_recv()
        across[k].append(send(at(2, 1, 0), k, 0, N, sibling))

    def all_here(k):
        for copy in across[k]:
            copy.wait_recv()

    def turn(weight, degree, first):
        for pair in range(BLOCKS // 2):
            for n in range(degree):
                tiles[pair, first + n] = jnp.transpose(
                    jnp.concatenate(
                        [weight[2 * pair, n].astype(F32), weight[2 * pair + 1, n].astype(F32)], axis=0
                    )
                ).astype(BF16)

    def build(links, count, degree, first, out):
        def pair_of(pair, carry):
            parts = [tiles[pair, first + n] for n in range(degree)]
            wanted = [
                jnp.where(low[0:1], links[n, 2 * pair], links[n, 2 * pair + 1])
                for n in range(degree)
            ]

            def source_blocks(g, c):
                for i in range(4):
                    r = g * 4 + i
                    terms = [
                        p * jnp.where(w == r, 1.0, 0.0).astype(BF16) for p, w in zip(parts, wanted)
                    ]
                    out[
                        pl.ds(pl.multiple_of(r * BS, BS), BS),
                        pl.ds(pl.multiple_of(pair * 128, 128), 128),
                    ] = functools.reduce(lambda u, v: u + v, terms)
                return c

            return lax.fori_loop(0, count // 4, source_blocks, carry)

        lax.fori_loop(0, BLOCKS // 2, pair_of, 0)

    def build_inverse():
        forth[...] = jnp.zeros_like(forth)
        back[...] = jnp.zeros_like(back)
        gap = jnp.zeros((BS, BS), F32)
        for b in range(BLOCKS):
            quad, place = b // 4, b % 4
            value = inverse_w[b].astype(F32)
            for out, tile in ((forth, jnp.transpose(value)), (back, value)):
                wide = jnp.concatenate([tile, gap] if place % 2 == 0 else [gap, tile], axis=1)
                lane = place // 2 * 128
                out[quad, place * BS : (place + 1) * BS, lane : lane + 128] = wide.astype(BF16)

    def couple_local(k):
        def part(r, carry):
            rows = pl.ds(pl.multiple_of(k * CHUNK_ROWS + r * SUB, SUB), SUB)
            for n in range(4):
                cols = slice(n * 256, (n + 1) * 256)
                total[rows, cols] = total[rows, cols] - jnp.dot(
                    ordered[rows, :], near[:, cols], preferred_element_type=F32
                )
            return carry

        lax.fori_loop(0, CHUNK_ROWS // SUB, part, 0)

    def couple_remote(k):
        def part(r, carry):
            rows = pl.ds(pl.multiple_of(k * CHUNK_ROWS + r * SUB, SUB), SUB)
            inner = pl.ds(pl.multiple_of(r * SUB, SUB), SUB)
            for n in range(4):
                cols = slice(n * 256, (n + 1) * 256)
                left = jnp.concatenate([shared[k, g, inner, :] for g in range(GROUPS)], axis=1)
                total[rows, cols] = total[rows, cols] - jnp.dot(
                    left, far[:, cols], preferred_element_type=F32
                )
            for n in range(4):
                cols = slice(n * 256, (n + 1) * 256)
                states[rows, cols] = jnp.dot(
                    total[rows, cols].astype(BF16), forth[n], preferred_element_type=F32
                )
            return carry

        lax.fori_loop(0, CHUNK_ROWS // SUB, part, 0)

    def scan_forward(k, state):
        def day(t, s):
            s = s * retain[pl.ds(t, 1), :] + states[day_rows(t), :] * active[pl.ds(t, 1), :]
            states[day_rows(t), :] = s
            return s

        return lax.fori_loop(k * CHUNK_DAYS, (k + 1) * CHUNK_DAYS, day, state)

    def prepare_decay():
        on = lax.broadcasted_iota(jnp.int32, (DAYS, WIDTH), 0) < slab_days[0]
        active[...] = jnp.where(on, 1.0, 0.0)
        retain[0:DAYS, :] = jnp.where(on, retention_ref[...], 1.0)
        retain[DAYS : DAYS + 8, :] = jnp.ones((8, WIDTH), F32)

        def ahead(t, d):
            d = d * retain[pl.ds(t, 1), :]
            forward_decay[pl.ds(t, 1), :] = d
            return d

        product = lax.fori_loop(0, DAYS, ahead, jnp.ones((1, WIDTH), F32))

        def behind(i, d):
            t = DAYS - 1 - i
            d = d * retain[pl.ds(t + 1, 1), :]
            backward_decay[pl.ds(t, 1), :] = d
            return d

        lax.fori_loop(0, DAYS, behind, jnp.ones((1, WIDTH), F32))
        for q in range(8):
            slab_decay[tm, q : q + 1, :] = product[:, q * 128 : (q + 1) * 128]

    def tm_copy(buf, kind, d):
        to = (tm + d) % SLABS if kind < 2 else (tm + SLABS - d) % SLABS
        return pltpu.make_async_remote_copy(
            src_ref=buf.at[tm],
            dst_ref=buf.at[tm],
            send_sem=tm_send.at[kind * 8 + d],
            recv_sem=tm_recv.at[kind * 8 + d],
            device_id=(to, space),
            device_id_type=MESH,
        )

    def same_row(other):
        return other // (SLABS // 2) == tm // (SLABS // 2)

    def exchange(kind, wide, narrow, act):
        for d in range(1, SLABS):
            ahead = (kind == 1) == (act != "wait_recv")
            other = tm + d if ahead else tm - d
            real = other < SLABS if ahead else other >= 0
            near_by = same_row(other)

            @pl.when(jnp.logical_and(real, near_by))
            def _():
                getattr(tm_copy(wide, kind, d), act)()

            @pl.when(jnp.logical_and(real, jnp.logical_not(near_by)))
            def _():
                getattr(tm_copy(narrow, kind, d), act)()

    def arrived(s, wide, narrow):
        return jnp.where(same_row(s), wide[s], narrow[s].astype(F32))

    def prepare_response():
        for n in range(4):
            cols = slice(n * 256, (n + 1) * 256)
            decay = forward_decay[:, cols]
            gram = lax.dot_general(
                decay * active[:, cols],
                decay,
                (((0,), (0,)), ((), ())),
                precision=lax.Precision.HIGHEST,
                preferred_element_type=F32,
            )
            response[n] = gram * back[n].astype(F32)

    def decay_of(s):
        return jnp.concatenate([slab_decay[s, q : q + 1, :] for q in range(8)], axis=1)

    for k in range(CHUNKS):
        fetch[k].wait()
    pick_shared()
    prepare_decay()
    pl.semaphore_wait(barrier, 4 + SLABS - 1)
    for k in range(CHUNKS):
        send_own(k)
    decay_copies = [tm_copy(slab_decay, 0, d) for d in range(1, SLABS)]
    for copy in decay_copies:
        copy.start()
    permute(0)
    permute(1)
    relay_first(0)
    order(0)
    relay_first(1)
    order(1)
    weights[0].wait()
    turn(local_w, 4, 0)
    build(local_links, BLOCKS, 4, 0, near)
    relay_second(0)
    weights[1].wait()
    turn(remote_w, 2, 4)
    build(remote_links, 2 * GROUPS, 2, 4, far)
    relay_second(1)
    couple_local(0)
    relay_third(0)
    couple_local(1)
    weights[2].wait()
    build_inverse()
    prepare_response()
    all_here(0)
    couple_remote(0)
    state = scan_forward(0, jnp.zeros((PROBES, WIDTH), F32))
    relay_third(1)
    all_here(1)
    couple_remote(1)
    state = scan_forward(1, state)
    ends[tm] = state
    ends_short[tm] = state.astype(BF16)
    exchange(1, ends, ends_short, "start")

    row8 = lax.broadcasted_iota(jnp.int32, (8, 128), 0)

    def fold(values):
        for step in (1, 2, 4):
            keep = (row8 & step) == 0
            values = [
                jnp.where(keep, u, v) + pltpu.roll(jnp.where(keep, v, u), step, 0)
                for u, v in zip(values[0::2], values[1::2])
            ]
        return values[0]

    def adjoint_sweep(carry, with_sums):
        def fix(g, c):
            for i in range(2):
                t = 2 * g + i
                value = states[day_rows(t), :]
                if with_sums:
                    value = value + forward_decay[pl.ds(t, 1), :] * c
                stored[day_rows(t), :] = value.astype(BF16)
            return c

        lax.fori_loop(0, DAYS // 2, fix, carry)

        def part(r, c):
            rows = pl.ds(pl.multiple_of(r * SUB, SUB), SUB)
            for n in range(4):
                cols = slice(n * 256, (n + 1) * 256)
                total[rows, cols] = jnp.dot(stored[rows, cols], back[n], preferred_element_type=F32)
            return c

        lax.fori_loop(0, ROWS // SUB, part, 0)
        leave = []
        for n in range(4):
            cols = slice(n * 256, (n + 1) * 256)

            def days(i, u):
                g = DAYS // 8 - 1 - i
                sums = [[None] * 8, [None] * 8]
                for j in reversed(range(8)):
                    t = g * 8 + j
                    u = total[day_rows(t), cols] * active[pl.ds(t, 1), cols] + retain[
                        pl.ds(t + 1, 1), cols
                    ] * u
                    if with_sums:
                        product = ordered[day_rows(t), cols].astype(F32) * u
                        for h in range(2):
                            half = product[:, h * 128 : (h + 1) * 128]
                            sums[h][j] = half[0:8] + half[8:16]
                if with_sums:
                    eight = pl.ds(pl.multiple_of(g * 8, 8), 8)
                    for h in range(2):
                        lane = n * 256 + h * 128
                        partial[eight, lane : lane + 128] = fold(sums[h])
                return u

            leave.append(
                lax.fori_loop(0, DAYS // 8, days, jnp.zeros((PROBES, 256), F32))
                * retain[0:1, cols]
            )
        return leave

    leave = adjoint_sweep(0, False)
    for copy in decay_copies:
        copy.wait_recv()
    exchange(1, ends, ends_short, "wait_recv")
    carry = jnp.zeros((PROBES, WIDTH), F32)
    for s in range(SLABS - 1):
        carry = jnp.where(s < tm, decay_of(s) * carry + arrived(s, ends, ends_short), carry)
    for n in range(4):
        cols = slice(n * 256, (n + 1) * 256)
        value = leave[n] + jnp.dot(
            carry[:, cols],
            response[n],
            precision=lax.Precision.HIGHEST,
            preferred_element_type=F32,
        )
        leaving[tm, :, cols] = value
        leaving_short[tm, :, cols] = value.astype(BF16)
    exchange(2, leaving, leaving_short, "start")
    adjoint_sweep(carry, True)

    for copy in pending:
        copy.wait_send()
    for copy in decay_copies:
        copy.wait_send()
    exchange(1, ends, ends_short, "wait_send")
    exchange(2, leaving, leaving_short, "wait_recv")

    carry = jnp.zeros((PROBES, WIDTH), F32)
    for s in reversed(range(1, SLABS)):
        carry = jnp.where(s > tm, decay_of(s) * carry + arrived(s, leaving, leaving_short), carry)

    for n in range(8):
        cols = slice(n * 128, (n + 1) * 128)
        part_carry = carry[:, cols]

        def finish(g, c):
            eight = pl.ds(pl.multiple_of(g * 8, 8), 8)
            z = ordered[pl.ds(pl.multiple_of(g * 128, 128), 128), cols].astype(F32)
            extra = fold(
                [
                    z[16 * d : 16 * d + 8] * c[0:8] + z[16 * d + 8 : 16 * d + 16] * c[8:16]
                    for d in range(8)
                ]
            )
            out_ref[eight, cols] = (partial[eight, cols] + backward_decay[eight, cols] * extra) * (
                1.0 / PROBES
            )
            return c

        lax.fori_loop(0, DAYS // 8, finish, part_carry)
    exchange(2, leaving, leaving_short, "wait_send")


def local(
    probes,
    local_links,
    remote_links,
    shared_blocks,
    slab_days,
    local_coupling,
    remote_coupling,
    block_inverse,
    retention,
):
    smem = pl.BlockSpec(memory_space=pltpu.SMEM)
    vmem = pl.BlockSpec(memory_space=pltpu.VMEM)
    anywhere = pl.BlockSpec(memory_space=pl.ANY)
    return pl.pallas_call(
        kernel,
        out_shape=jax.ShapeDtypeStruct((DAYS, WIDTH), F32),
        in_specs=[smem] * 4 + [anywhere] * 4 + [vmem],
        out_specs=vmem,
        scratch_shapes=[
            pltpu.VMEM((ROWS, WIDTH), BF16),
            pltpu.VMEM(local_coupling.shape, BF16),
            pltpu.VMEM(remote_coupling.shape, BF16),
            pltpu.VMEM(block_inverse.shape, BF16),
            pltpu.VMEM((WIDTH, WIDTH), BF16),
            pltpu.VMEM((ROWS * 8, 128), F32),
            pltpu.VMEM((2 * DAYS, WIDTH), BF16),
            pltpu.VMEM((2 * DAYS * 8, 128), F32),
            pltpu.VMEM((ROWS, WIDTH), BF16),
            pltpu.VMEM((CHUNKS, GROUPS, CHUNK_ROWS, 128), BF16),
            pltpu.VMEM((BLOCKS // 2, 6, BS, 128), BF16),
            pltpu.VMEM((WIDTH, WIDTH), BF16),
            pltpu.VMEM((2 * WIDTH, WIDTH), BF16),
            pltpu.VMEM((4, 256, 256), BF16),
            pltpu.VMEM((4, 256, 256), BF16),
            pltpu.VMEM((ROWS, WIDTH), F32),
            pltpu.VMEM((ROWS, WIDTH), F32),
            pltpu.VMEM((ROWS, WIDTH), BF16),
            pltpu.VMEM((DAYS + 8, WIDTH), F32),
            pltpu.VMEM((DAYS, WIDTH), F32),
            pltpu.VMEM((DAYS, WIDTH), F32),
            pltpu.VMEM((DAYS, WIDTH), F32),
            pltpu.VMEM((DAYS, WIDTH), F32),
            pltpu.VMEM((SLABS, 8, 128), F32),
            pltpu.VMEM((4, 256, 256), F32),
            pltpu.VMEM((SLABS, PROBES, WIDTH), F32),
            pltpu.VMEM((SLABS, PROBES, WIDTH), BF16),
            pltpu.VMEM((SLABS, PROBES, WIDTH), F32),
            pltpu.VMEM((SLABS, PROBES, WIDTH), BF16),
            pltpu.SemaphoreType.DMA((CHUNKS + 3,)),
            pltpu.SemaphoreType.DMA((CHUNKS * 20,)),
            pltpu.SemaphoreType.DMA((CHUNKS * 20,)),
            pltpu.SemaphoreType.DMA((24,)),
            pltpu.SemaphoreType.DMA((24,)),
        ],
        compiler_params=pltpu.CompilerParams(
            vmem_limit_bytes=60 << 20, collective_id=0, has_side_effects=True
        ),
    )(
        local_links.T,
        remote_links.T,
        shared_blocks,
        slab_days,
        probes.reshape(ROWS, WIDTH),
        local_coupling,
        remote_coupling,
        block_inverse,
        retention,
    )


def solution(mesh):
    placed = (
        P("tm", "space", None),
        P("space", None),
        P("space", None),
        P("space", None),
        P("tm"),
        P("space", None, None, None),
        P("space", None, None, None),
        P("space", None, None),
        P("tm", "space"),
    )
    return jax.shard_map(
        local, mesh=mesh, in_specs=placed, out_specs=P("tm", "space"), check_vma=False
    )
```

```python
import functools

import jax
import jax.numpy as jnp
from jax import lax
from jax.experimental import pallas as pl
from jax.experimental.pallas import tpu as pltpu
from jax.sharding import PartitionSpec as P

F32, BF16 = jnp.float32, jnp.bfloat16
MESH = pl.DeviceIdType.MESH
DAYS, BLOCKS, BS, PROBES, GROUPS, SLABS = 48, 16, 64, 16, 16, 8
WIDTH = BLOCKS * BS
ROWS = DAYS * PROBES
CHUNKS = 2
CHUNK_ROWS = ROWS // CHUNKS
CHUNK_DAYS = DAYS // CHUNKS
HALF = CHUNK_ROWS // 2
SUB = 192


def day_rows(t):
    return pl.ds(pl.multiple_of(t * PROBES, PROBES), PROBES)


def kernel(
    local_links,
    remote_links,
    shared_blocks,
    slab_days,
    probes_hbm,
    local_hbm,
    remote_hbm,
    inverse_hbm,
    retention_ref,
    out_ref,
    probes,
    local_w,
    remote_w,
    inverse_w,
    shuffle,
    shuffled,
    picked,
    picked_shuffled,
    ordered,
    shared,
    tiles,
    near,
    far,
    forth,
    back,
    total,
    states,
    stored,
    retain,
    active,
    forward_decay,
    backward_decay,
    partial,
    slab_decay,
    response,
    ends,
    ends_short,
    leaving,
    leaving_short,
    in_sem,
    send_sem,
    recv_sem,
    tm_send,
    tm_recv,
):
    tm = lax.axis_index("tm")
    space = lax.axis_index("space")
    core, x, y = space % 2, (space // 2) % 4, space // 8

    def at(dx, dy, dc):
        return ((y + dy) % 2 * 4 + (x + dx) % 4) * 2 + (core + dc) % 2

    me = at(0, 0, 0)
    sibling = at(0, 0, 1)

    barrier = pltpu.get_barrier_semaphore()
    for to in (at(1, 0, 0), at(3, 0, 0), at(0, 1, 0), sibling):
        pl.semaphore_signal(barrier, inc=1, device_id=(tm, to), device_id_type=MESH)
    for d in range(1, SLABS):
        pl.semaphore_signal(
            barrier, inc=1, device_id=((tm + d) % SLABS, space), device_id_type=MESH
        )

    fetch = []
    for k in range(CHUNKS):
        rows = pl.ds(k * CHUNK_ROWS, CHUNK_ROWS)
        fetch.append(pltpu.make_async_copy(probes_hbm.at[rows], probes.at[rows], in_sem.at[k]))
    weights = [
        pltpu.make_async_copy(local_hbm, local_w, in_sem.at[CHUNKS]),
        pltpu.make_async_copy(remote_hbm, remote_w, in_sem.at[CHUNKS + 1]),
        pltpu.make_async_copy(inverse_hbm, inverse_w, in_sem.at[CHUNKS + 2]),
    ]
    for copy in fetch:
        copy.start()

    def shuffle_rows(r, carry):
        source = lax.broadcasted_iota(jnp.int32, (64, 128), 0) + r * 64
        gap = (source & (PROBES - 1)) * BS + (source >> 4)
        gap = gap - lax.broadcasted_iota(jnp.int32, (64, 128), 1)
        for q in range(8):
            shuffle[pl.ds(pl.multiple_of(r * 64, 64), 64), q * 128 : (q + 1) * 128] = jnp.where(
                gap == q * 128, 1.0, 0.0
            ).astype(BF16)
        return carry

    lax.fori_loop(0, WIDTH // 64, shuffle_rows, 0)

    low = lax.broadcasted_iota(jnp.int32, (8, 128), 1) < BS

    def pair_up(first, second):
        mixed = pltpu.roll(jnp.where(low, second, first), BS, 1)
        return jnp.concatenate(
            [jnp.where(low, first, mixed), jnp.where(low, mixed, second)], axis=0
        )

    def block_row(t, b):
        return shuffled[pl.ds(pl.multiple_of((t * BLOCKS + b) * 8, 8), 8), :]

    def permute(k):
        def part(r, carry):
            lo = k * CHUNK_ROWS + r * SUB
            for n in range(4):
                value = jnp.dot(
                    probes[pl.ds(pl.multiple_of(lo, SUB), SUB), :],
                    shuffle[:, n * 256 : (n + 1) * 256],
                    preferred_element_type=F32,
                )
                for h in range(2):
                    shuffled[pl.ds(lo * 8 + 2 * n + h, SUB, stride=8), :] = value[
                        :, h * 128 : (h + 1) * 128
                    ]
            return carry

        lax.fori_loop(0, CHUNK_ROWS // SUB, part, 0)

    def pick_shared():
        row = lax.broadcasted_iota(jnp.int32, (2 * DAYS, ROWS), 0)
        column = lax.broadcasted_iota(jnp.int32, (2 * DAYS, ROWS), 1)
        second = row >= DAYS
        day = jnp.where(second, row - DAYS, row)
        wanted = day * BLOCKS + jnp.where(second, shared_blocks[0, 1], shared_blocks[0, 0])
        select = jnp.where(column == wanted, 1.0, 0.0).astype(BF16)
        for n in range(4):
            cols = slice(n * 256, (n + 1) * 256)
            picked[:, cols] = jnp.dot(
                select, probes[:, cols], preferred_element_type=F32
            ).astype(BF16)
        for n in range(4):
            value = jnp.dot(
                picked[...], shuffle[:, n * 256 : (n + 1) * 256], preferred_element_type=F32
            )
            for h in range(2):
                picked_shuffled[pl.ds(2 * n + h, 2 * DAYS, stride=8), :] = value[
                    :, h * 128 : (h + 1) * 128
                ]

        def days(g, carry):
            for i in range(4):
                t = g * 4 + i
                tiles = [
                    picked_shuffled[pl.ds(pl.multiple_of((m * DAYS + t) * 8, 8), 8), :]
                    for m in range(2)
                ]
                shared[t // CHUNK_DAYS, me, day_rows(t % CHUNK_DAYS), :] = pair_up(*tiles).astype(BF16)
            return carry

        lax.fori_loop(0, DAYS // 4, days, 0)

    def order(k):
        def days(g, carry):
            for i in range(4):
                t = g * 4 + i
                for pair in range(BLOCKS // 2):
                    value = pair_up(block_row(t, 2 * pair), block_row(t, 2 * pair + 1))
                    total[day_rows(t), pair * 128 : (pair + 1) * 128] = value
                    ordered[day_rows(t), pair * 128 : (pair + 1) * 128] = value.astype(BF16)
            return carry

        lax.fori_loop(k * CHUNK_DAYS // 4, (k + 1) * CHUNK_DAYS // 4, days, 0)

    used = [0]
    pending = []

    def send(slot, k, lo, rows, to):
        i = used[0]
        used[0] += 1
        where = shared.at[k, slot, pl.ds(lo, rows)]
        copy = pltpu.make_async_remote_copy(
            src_ref=where,
            dst_ref=where,
            send_sem=send_sem.at[i],
            recv_sem=recv_sem.at[i],
            device_id=(tm, to),
            device_id_type=MESH,
        )
        copy.start()
        pending.append(copy)
        return copy

    flows = [{} for _ in range(CHUNKS)]
    across = {"near": [], "middle": [], "last": []}
    N = CHUNK_ROWS

    def send_own(k):
        f = flows[k]
        f["y"] = send(me, k, 0, N, at(0, 1, 0))
        f["p0"] = send(me, k, 0, N, at(1, 0, 0))
        f["m0"] = send(me, k, 0, N, at(3, 0, 0))
        across["near"].append(send(me, k, 0, N, sibling))

    def relay_first(k):
        f = flows[k]
        f["y"].wait_recv()
        f["p1"] = send(at(0, 1, 0), k, 0, N, at(1, 0, 0))
        f["m1"] = send(at(0, 1, 0), k, 0, N, at(3, 0, 0))
        across["near"].append(send(at(0, 1, 0), k, 0, N, sibling))
        f["p0"].wait_recv()
        f["pp0"] = send(at(3, 0, 0), k, 0, HALF, at(1, 0, 0))
        across["near"].append(send(at(3, 0, 0), k, 0, N, sibling))
        f["m0"].wait_recv()
        f["mm0"] = send(at(1, 0, 0), k, HALF, HALF, at(3, 0, 0))
        across["near"].append(send(at(1, 0, 0), k, 0, N, sibling))

    def relay_second(k):
        f = flows[k]
        f["p1"].wait_recv()
        f["pp1"] = send(at(3, 1, 0), k, 0, HALF, at(1, 0, 0))
        across["middle"].append(send(at(3, 1, 0), k, 0, N, sibling))
        f["m1"].wait_recv()
        f["mm1"] = send(at(1, 1, 0), k, HALF, HALF, at(3, 0, 0))
        across["middle"].append(send(at(1, 1, 0), k, 0, N, sibling))

    def relay_third(k):
        f = flows[k]
        f["pp0"].wait_recv()
        f["mm0"].wait_recv()
        across["middle"].append(send(at(2, 0, 0), k, 0, N, sibling))

    def relay_fourth(k):
        f = flows[k]
        f["pp1"].wait_recv()
        f["mm1"].wait_recv()
        across["last"].append(send(at(2, 1, 0), k, 0, N, sibling))

    def all_here(stage):
        for copy in across[stage]:
            copy.wait_recv()

    def turn(weight, degree, first):
        for pair in range(BLOCKS // 2):
            for n in range(degree):
                tiles[pair, first + n] = jnp.transpose(
                    jnp.concatenate(
                        [weight[2 * pair, n].astype(F32), weight[2 * pair + 1, n].astype(F32)], axis=0
                    )
                ).astype(BF16)

    def build(links, count, degree, first, out):
        def pair_of(pair, carry):
            parts = [tiles[pair, first + n] for n in range(degree)]
            wanted = [
                jnp.where(low[0:1], links[n, 2 * pair], links[n, 2 * pair + 1])
                for n in range(degree)
            ]

            def source_blocks(g, c):
                for i in range(4):
                    r = g * 4 + i
                    terms = [
                        p * jnp.where(w == r, 1.0, 0.0).astype(BF16) for p, w in zip(parts, wanted)
                    ]
                    out[
                        pl.ds(pl.multiple_of(r * BS, BS), BS),
                        pl.ds(pl.multiple_of(pair * 128, 128), 128),
                    ] = functools.reduce(lambda u, v: u + v, terms)
                return c

            return lax.fori_loop(0, count // 4, source_blocks, carry)

        lax.fori_loop(0, BLOCKS // 2, pair_of, 0)

    def build_inverse():
        forth[...] = jnp.zeros_like(forth)
        back[...] = jnp.zeros_like(back)
        gap = jnp.zeros((BS, BS), F32)
        for b in range(BLOCKS):
            quad, place = b // 4, b % 4
            value = inverse_w[b].astype(F32)
            for out, tile in ((forth, jnp.transpose(value)), (back, value)):
                wide = jnp.concatenate([tile, gap] if place % 2 == 0 else [gap, tile], axis=1)
                lane = place // 2 * 128
                out[quad, place * BS : (place + 1) * BS, lane : lane + 128] = wide.astype(BF16)

    def couple_local():
        def part(r, carry):
            rows = pl.ds(pl.multiple_of(r * SUB, SUB), SUB)
            for n in range(4):
                cols = slice(n * 256, (n + 1) * 256)
                total[rows, cols] = total[rows, cols] - jnp.dot(
                    ordered[rows, :], near[:, cols], preferred_element_type=F32
                )
            return carry

        lax.fori_loop(0, ROWS // SUB, part, 0)

    def couple_remote(*chips):
        places = [at(dx, dy, 0) // 2 for dx, dy in chips]

        def part(r, carry):
            rows = pl.ds(pl.multiple_of(r * SUB, SUB), SUB)
            k = r // (CHUNK_ROWS // SUB)
            inner = pl.ds(pl.multiple_of(r % (CHUNK_ROWS // SUB) * SUB, SUB), SUB)
            for n in range(4):
                cols = slice(n * 256, (n + 1) * 256)
                left = jnp.concatenate(
                    [shared[k, 2 * q + c, inner, :] for q in places for c in range(2)], axis=1
                )
                right = jnp.concatenate(
                    [far[pl.ds(pl.multiple_of(q * 256, 256), 256), cols] for q in places], axis=0
                )
                total[rows, cols] = total[rows, cols] - jnp.dot(
                    left, right, preferred_element_type=F32
                )
            return carry

        lax.fori_loop(0, ROWS // SUB, part, 0)

    def force():
        def part(r, carry):
            rows = pl.ds(pl.multiple_of(r * SUB, SUB), SUB)
            for n in range(4):
                cols = slice(n * 256, (n + 1) * 256)
                states[rows, cols] = jnp.dot(
                    total[rows, cols].astype(BF16), forth[n], preferred_element_type=F32
                )
            return carry

        lax.fori_loop(0, ROWS // SUB, part, 0)

    def scan_forward(k, state):
        def day(t, s):
            s = s * retain[pl.ds(t, 1), :] + states[day_rows(t), :] * active[pl.ds(t, 1), :]
            states[day_rows(t), :] = s
            return s

        return lax.fori_loop(k * CHUNK_DAYS, (k + 1) * CHUNK_DAYS, day, state)

    def prepare_decay():
        on = lax.broadcasted_iota(jnp.int32, (DAYS, WIDTH), 0) < slab_days[0]
        active[...] = jnp.where(on, 1.0, 0.0)
        retain[0:DAYS, :] = jnp.where(on, retention_ref[...], 1.0)
        retain[DAYS : DAYS + 8, :] = jnp.ones((8, WIDTH), F32)

        def ahead(t, d):
            d = d * retain[pl.ds(t, 1), :]
            forward_decay[pl.ds(t, 1), :] = d
            return d

        product = lax.fori_loop(0, DAYS, ahead, jnp.ones((1, WIDTH), F32))

        def behind(i, d):
            t = DAYS - 1 - i
            d = d * retain[pl.ds(t + 1, 1), :]
            backward_decay[pl.ds(t, 1), :] = d
            return d

        lax.fori_loop(0, DAYS, behind, jnp.ones((1, WIDTH), F32))
        for q in range(8):
            slab_decay[tm, q : q + 1, :] = product[:, q * 128 : (q + 1) * 128]

    def tm_copy(buf, to, send, recv):
        return pltpu.make_async_remote_copy(
            src_ref=buf.at[tm],
            dst_ref=buf.at[tm],
            send_sem=tm_send.at[send],
            recv_sem=tm_recv.at[recv],
            device_id=(to, space),
            device_id_type=MESH,
        )

    def same_row(other):
        return other // (SLABS // 2) == tm // (SLABS // 2)

    def exchange(kind, wide, narrow, act):
        for d in reversed(range(1, SLABS)):
            ahead = (kind == 1) == (act != "wait_recv")
            other = tm + d if ahead else tm - d
            real = other < SLABS if ahead else other >= 0
            near_by = same_row(other)

            peer = (other + SLABS) % SLABS
            signal = peer if act == "wait_recv" else tm

            @pl.when(jnp.logical_and(real, near_by))
            def _():
                getattr(tm_copy(wide, peer, peer, signal), act)()

            @pl.when(jnp.logical_and(real, jnp.logical_not(near_by)))
            def _():
                getattr(tm_copy(narrow, peer, peer, signal), act)()

    def arrived(s, wide, narrow):
        return jnp.where(same_row(s), wide[s], narrow[s].astype(F32))

    def prepare_response():
        for n in range(4):
            cols = slice(n * 256, (n + 1) * 256)
            decay = forward_decay[:, cols]
            gram = lax.dot_general(
                decay * active[:, cols],
                decay,
                (((0,), (0,)), ((), ())),
                precision=lax.Precision.HIGHEST,
                preferred_element_type=F32,
            )
            response[n] = gram * back[n].astype(F32)

    def decay_of(s):
        return jnp.concatenate([slab_decay[s, q : q + 1, :] for q in range(8)], axis=1)

    for k in range(CHUNKS):
        fetch[k].wait()
    pick_shared()
    for copy in weights:
        copy.start()
    pl.semaphore_wait(barrier, 4 + SLABS - 1)
    for k in range(CHUNKS):
        send_own(k)
    prepare_decay()
    decay_copies = [
        tm_copy(slab_decay, (tm + d) % SLABS, SLABS + d - 1, SLABS + d - 1)
        for d in range(1, SLABS)
    ]
    for copy in decay_copies:
        copy.start()
    permute(0)
    permute(1)
    order(0)
    order(1)
    weights[0].wait()
    weights[1].wait()
    turn(local_w, 4, 0)
    turn(remote_w, 2, 4)
    relay_first(0)
    relay_first(1)
    build(local_links, BLOCKS, 4, 0, near)
    build(remote_links, 2 * GROUPS, 2, 4, far)
    couple_local()
    relay_second(0)
    relay_second(1)
    all_here("near")
    couple_remote((0, 0), (1, 0), (3, 0), (0, 1))
    relay_third(0)
    relay_third(1)
    weights[2].wait()
    build_inverse()
    prepare_response()
    all_here("middle")
    couple_remote((2, 0), (1, 1), (3, 1))
    relay_fourth(0)
    relay_fourth(1)
    all_here("last")
    couple_remote((2, 1))
    force()
    state = scan_forward(0, jnp.zeros((PROBES, WIDTH), F32))
    state = scan_forward(1, state)
    ends[tm] = state
    ends_short[tm] = state.astype(BF16)
    exchange(1, ends, ends_short, "start")

    row8 = lax.broadcasted_iota(jnp.int32, (8, 128), 0)

    def fold(values):
        for step in (1, 2, 4):
            keep = (row8 & step) == 0
            values = [
                jnp.where(keep, u, v) + pltpu.roll(jnp.where(keep, v, u), step, 0)
                for u, v in zip(values[0::2], values[1::2])
            ]
        return values[0]

    def adjoint_sweep(carry, with_sums):
        def fix(g, c):
            for i in range(2):
                t = 2 * g + i
                value = states[day_rows(t), :]
                if with_sums:
                    value = value + forward_decay[pl.ds(t, 1), :] * c
                stored[day_rows(t), :] = value.astype(BF16)
            return c

        lax.fori_loop(0, DAYS // 2, fix, carry)

        def part(r, c):
            rows = pl.ds(pl.multiple_of(r * SUB, SUB), SUB)
            for n in range(4):
                cols = slice(n * 256, (n + 1) * 256)
                total[rows, cols] = jnp.dot(stored[rows, cols], back[n], preferred_element_type=F32)
            return c

        lax.fori_loop(0, ROWS // SUB, part, 0)
        leave = []
        for n in range(4):
            cols = slice(n * 256, (n + 1) * 256)

            def days(i, u):
                g = DAYS // 8 - 1 - i
                sums = [[None] * 8, [None] * 8]
                for j in reversed(range(8)):
                    t = g * 8 + j
                    u = total[day_rows(t), cols] * active[pl.ds(t, 1), cols] + retain[
                        pl.ds(t + 1, 1), cols
                    ] * u
                    if with_sums:
                        product = ordered[day_rows(t), cols].astype(F32) * u
                        for h in range(2):
                            half = product[:, h * 128 : (h + 1) * 128]
                            sums[h][j] = half[0:8] + half[8:16]
                if with_sums:
                    eight = pl.ds(pl.multiple_of(g * 8, 8), 8)
                    for h in range(2):
                        lane = n * 256 + h * 128
                        partial[eight, lane : lane + 128] = fold(sums[h])
                return u

            leave.append(
                lax.fori_loop(0, DAYS // 8, days, jnp.zeros((PROBES, 256), F32))
                * retain[0:1, cols]
            )
        return leave

    leave = adjoint_sweep(0, False)
    for copy in decay_copies:
        copy.wait_recv()
    exchange(1, ends, ends_short, "wait_recv")
    carry = jnp.zeros((PROBES, WIDTH), F32)
    for s in range(SLABS - 1):
        carry = jnp.where(s < tm, decay_of(s) * carry + arrived(s, ends, ends_short), carry)
    for n in range(4):
        cols = slice(n * 256, (n + 1) * 256)
        value = leave[n] + jnp.dot(
            carry[:, cols],
            response[n],
            precision=lax.Precision.HIGHEST,
            preferred_element_type=F32,
        )
        leaving[tm, :, cols] = value
        leaving_short[tm, :, cols] = value.astype(BF16)
    exchange(2, leaving, leaving_short, "start")
    adjoint_sweep(carry, True)

    for copy in pending:
        copy.wait_send()
    for copy in decay_copies:
        copy.wait_send()
    exchange(1, ends, ends_short, "wait_send")
    exchange(2, leaving, leaving_short, "wait_recv")

    carry = jnp.zeros((PROBES, WIDTH), F32)
    for s in reversed(range(1, SLABS)):
        carry = jnp.where(s > tm, decay_of(s) * carry + arrived(s, leaving, leaving_short), carry)

    for n in range(8):
        cols = slice(n * 128, (n + 1) * 128)
        part_carry = carry[:, cols]

        def finish(g, c):
            eight = pl.ds(pl.multiple_of(g * 8, 8), 8)
            z = ordered[pl.ds(pl.multiple_of(g * 128, 128), 128), cols].astype(F32)
            extra = fold(
                [
                    z[16 * d : 16 * d + 8] * c[0:8] + z[16 * d + 8 : 16 * d + 16] * c[8:16]
                    for d in range(8)
                ]
            )
            out_ref[eight, cols] = (partial[eight, cols] + backward_decay[eight, cols] * extra) * (
                1.0 / PROBES
            )
            return c

        lax.fori_loop(0, DAYS // 8, finish, part_carry)
    exchange(2, leaving, leaving_short, "wait_send")


def local(
    probes,
    local_links,
    remote_links,
    shared_blocks,
    slab_days,
    local_coupling,
    remote_coupling,
    block_inverse,
    retention,
):
    smem = pl.BlockSpec(memory_space=pltpu.SMEM)
    vmem = pl.BlockSpec(memory_space=pltpu.VMEM)
    anywhere = pl.BlockSpec(memory_space=pl.ANY)
    return pl.pallas_call(
        kernel,
        out_shape=jax.ShapeDtypeStruct((DAYS, WIDTH), F32),
        in_specs=[smem] * 4 + [anywhere] * 4 + [vmem],
        out_specs=vmem,
        scratch_shapes=[
            pltpu.VMEM((ROWS, WIDTH), BF16),
            pltpu.VMEM(local_coupling.shape, BF16),
            pltpu.VMEM(remote_coupling.shape, BF16),
            pltpu.VMEM(block_inverse.shape, BF16),
            pltpu.VMEM((WIDTH, WIDTH), BF16),
            pltpu.VMEM((ROWS * 8, 128), F32),
            pltpu.VMEM((2 * DAYS, WIDTH), BF16),
            pltpu.VMEM((2 * DAYS * 8, 128), F32),
            pltpu.VMEM((ROWS, WIDTH), BF16),
            pltpu.VMEM((CHUNKS, GROUPS, CHUNK_ROWS, 128), BF16),
            pltpu.VMEM((BLOCKS // 2, 6, BS, 128), BF16),
            pltpu.VMEM((WIDTH, WIDTH), BF16),
            pltpu.VMEM((2 * WIDTH, WIDTH), BF16),
            pltpu.VMEM((4, 256, 256), BF16),
            pltpu.VMEM((4, 256, 256), BF16),
            pltpu.VMEM((ROWS, WIDTH), F32),
            pltpu.VMEM((ROWS, WIDTH), F32),
            pltpu.VMEM((ROWS, WIDTH), BF16),
            pltpu.VMEM((DAYS + 8, WIDTH), F32),
            pltpu.VMEM((DAYS, WIDTH), F32),
            pltpu.VMEM((DAYS, WIDTH), F32),
            pltpu.VMEM((DAYS, WIDTH), F32),
            pltpu.VMEM((DAYS, WIDTH), F32),
            pltpu.VMEM((SLABS, 8, 128), F32),
            pltpu.VMEM((4, 256, 256), F32),
            pltpu.VMEM((SLABS, PROBES, WIDTH), F32),
            pltpu.VMEM((SLABS, PROBES, WIDTH), BF16),
            pltpu.VMEM((SLABS, PROBES, WIDTH), F32),
            pltpu.VMEM((SLABS, PROBES, WIDTH), BF16),
            pltpu.SemaphoreType.DMA((CHUNKS + 3,)),
            pltpu.SemaphoreType.DMA((CHUNKS * 17,)),
            pltpu.SemaphoreType.DMA((CHUNKS * 17,)),
            pltpu.SemaphoreType.DMA((2 * SLABS - 1,)),
            pltpu.SemaphoreType.DMA((2 * SLABS - 1,)),
        ],
        compiler_params=pltpu.CompilerParams(
            vmem_limit_bytes=60 << 20, collective_id=0, has_side_effects=True
        ),
    )(
        local_links.T,
        remote_links.T,
        shared_blocks,
        slab_days,
        probes.reshape(ROWS, WIDTH),
        local_coupling,
        remote_coupling,
        block_inverse,
        retention,
    )


def solution(mesh):
    placed = (
        P("tm", "space", None),
        P("space", None),
        P("space", None),
        P("space", None),
        P("tm"),
        P("space", None, None, None),
        P("space", None, None, None),
        P("space", None, None),
        P("tm", "space"),
    )
    return jax.shard_map(
        local, mesh=mesh, in_specs=placed, out_specs=P("tm", "space"), check_vma=False
    )
```

```python
import functools

import jax
import jax.numpy as jnp
from jax import lax
from jax.experimental import pallas as pl
from jax.experimental.pallas import tpu as pltpu
from jax.sharding import PartitionSpec as P

F32, BF16 = jnp.float32, jnp.bfloat16
MESH = pl.DeviceIdType.MESH
DAYS, BLOCKS, BS, PROBES, GROUPS, SLABS = 48, 16, 64, 16, 16, 8
WIDTH = BLOCKS * BS
ROWS = DAYS * PROBES
CHUNKS = 2
CHUNK_ROWS = ROWS // CHUNKS
CHUNK_DAYS = DAYS // CHUNKS
HALF = CHUNK_ROWS // 2
SUB = 192


def day_rows(t):
    return pl.ds(pl.multiple_of(t * PROBES, PROBES), PROBES)


def kernel(
    local_links,
    remote_links,
    shared_blocks,
    slab_days,
    probes_hbm,
    local_hbm,
    remote_hbm,
    inverse_hbm,
    retention_ref,
    out_ref,
    probes,
    local_w,
    remote_w,
    inverse_w,
    shuffle,
    shuffled,
    picked,
    picked_shuffled,
    ordered,
    shared,
    tiles,
    near,
    far,
    forth,
    back,
    total,
    states,
    stored,
    retain,
    active,
    forward_decay,
    backward_decay,
    partial,
    slab_decay,
    response,
    ends,
    leaving,
    in_sem,
    send_sem,
    recv_sem,
    tm_send,
    tm_recv,
):
    tm = lax.axis_index("tm")
    space = lax.axis_index("space")
    core, x, y = space % 2, (space // 2) % 4, space // 8

    def at(dx, dy, dc):
        return ((y + dy) % 2 * 4 + (x + dx) % 4) * 2 + (core + dc) % 2

    me = at(0, 0, 0)
    sibling = at(0, 0, 1)

    barrier = pltpu.get_barrier_semaphore()
    for to in (at(1, 0, 0), at(3, 0, 0), at(0, 1, 0), sibling):
        pl.semaphore_signal(barrier, inc=1, device_id=(tm, to), device_id_type=MESH)
    for d in range(1, SLABS):
        pl.semaphore_signal(
            barrier, inc=1, device_id=((tm + d) % SLABS, space), device_id_type=MESH
        )

    fetch = []
    for k in range(CHUNKS):
        rows = pl.ds(k * CHUNK_ROWS, CHUNK_ROWS)
        fetch.append(pltpu.make_async_copy(probes_hbm.at[rows], probes.at[rows], in_sem.at[k]))
    weights = [
        pltpu.make_async_copy(local_hbm, local_w, in_sem.at[CHUNKS]),
        pltpu.make_async_copy(remote_hbm, remote_w, in_sem.at[CHUNKS + 1]),
        pltpu.make_async_copy(inverse_hbm, inverse_w, in_sem.at[CHUNKS + 2]),
    ]
    for copy in fetch:
        copy.start()

    def shuffle_rows(r, carry):
        source = lax.broadcasted_iota(jnp.int32, (64, 128), 0) + r * 64
        gap = (source & (PROBES - 1)) * BS + (source >> 4)
        gap = gap - lax.broadcasted_iota(jnp.int32, (64, 128), 1)
        for q in range(8):
            shuffle[pl.ds(pl.multiple_of(r * 64, 64), 64), q * 128 : (q + 1) * 128] = jnp.where(
                gap == q * 128, 1.0, 0.0
            ).astype(BF16)
        return carry

    lax.fori_loop(0, WIDTH // 64, shuffle_rows, 0)

    low = lax.broadcasted_iota(jnp.int32, (8, 128), 1) < BS

    def pair_up(first, second):
        mixed = pltpu.roll(jnp.where(low, second, first), BS, 1)
        return jnp.concatenate(
            [jnp.where(low, first, mixed), jnp.where(low, mixed, second)], axis=0
        )

    def block_row(t, b):
        return shuffled[pl.ds(pl.multiple_of((t * BLOCKS + b) * 8, 8), 8), :]

    def permute(k):
        def part(r, carry):
            lo = k * CHUNK_ROWS + r * SUB
            for n in range(4):
                value = jnp.dot(
                    probes[pl.ds(pl.multiple_of(lo, SUB), SUB), :],
                    shuffle[:, n * 256 : (n + 1) * 256],
                    preferred_element_type=F32,
                )
                for h in range(2):
                    shuffled[pl.ds(lo * 8 + 2 * n + h, SUB, stride=8), :] = value[
                        :, h * 128 : (h + 1) * 128
                    ]
            return carry

        lax.fori_loop(0, CHUNK_ROWS // SUB, part, 0)

    def pick_shared():
        row = lax.broadcasted_iota(jnp.int32, (2 * DAYS, ROWS), 0)
        column = lax.broadcasted_iota(jnp.int32, (2 * DAYS, ROWS), 1)
        second = row >= DAYS
        day = jnp.where(second, row - DAYS, row)
        wanted = day * BLOCKS + jnp.where(second, shared_blocks[0, 1], shared_blocks[0, 0])
        select = jnp.where(column == wanted, 1.0, 0.0).astype(BF16)
        for n in range(4):
            cols = slice(n * 256, (n + 1) * 256)
            picked[:, cols] = jnp.dot(
                select, probes[:, cols], preferred_element_type=F32
            ).astype(BF16)
        for n in range(4):
            value = jnp.dot(
                picked[...], shuffle[:, n * 256 : (n + 1) * 256], preferred_element_type=F32
            )
            for h in range(2):
                picked_shuffled[pl.ds(2 * n + h, 2 * DAYS, stride=8), :] = value[
                    :, h * 128 : (h + 1) * 128
                ]

        def days(g, carry):
            for i in range(4):
                t = g * 4 + i
                tiles = [
                    picked_shuffled[pl.ds(pl.multiple_of((m * DAYS + t) * 8, 8), 8), :]
                    for m in range(2)
                ]
                shared[t // CHUNK_DAYS, me, day_rows(t % CHUNK_DAYS), :] = pair_up(*tiles).astype(BF16)
            return carry

        lax.fori_loop(0, DAYS // 4, days, 0)

    def order(k):
        def days(g, carry):
            for i in range(4):
                t = g * 4 + i
                for pair in range(BLOCKS // 2):
                    value = pair_up(block_row(t, 2 * pair), block_row(t, 2 * pair + 1))
                    total[day_rows(t), pair * 128 : (pair + 1) * 128] = value
                    ordered[day_rows(t), pair * 128 : (pair + 1) * 128] = value.astype(BF16)
            return carry

        lax.fori_loop(k * CHUNK_DAYS // 4, (k + 1) * CHUNK_DAYS // 4, days, 0)

    used = [0]
    pending = []

    def send(slot, k, lo, rows, to):
        i = used[0]
        used[0] += 1
        where = shared.at[k, slot, pl.ds(lo, rows)]
        copy = pltpu.make_async_remote_copy(
            src_ref=where,
            dst_ref=where,
            send_sem=send_sem.at[i],
            recv_sem=recv_sem.at[i],
            device_id=(tm, to),
            device_id_type=MESH,
        )
        copy.start()
        pending.append(copy)
        return copy

    flows = [{} for _ in range(CHUNKS)]
    across = {"near": [], "middle": [], "last": []}
    N = CHUNK_ROWS

    def send_own(k):
        f = flows[k]
        f["y"] = send(me, k, 0, N, at(0, 1, 0))
        f["p0"] = send(me, k, 0, N, at(1, 0, 0))
        f["m0"] = send(me, k, 0, N, at(3, 0, 0))
        across["near"].append(send(me, k, 0, N, sibling))

    def relay_first(k):
        f = flows[k]
        f["y"].wait_recv()
        f["p1"] = send(at(0, 1, 0), k, 0, N, at(1, 0, 0))
        f["m1"] = send(at(0, 1, 0), k, 0, N, at(3, 0, 0))
        across["near"].append(send(at(0, 1, 0), k, 0, N, sibling))

    def relay_own_row(k):
        f = flows[k]
        f["p0"].wait_recv()
        f["pp0"] = send(at(3, 0, 0), k, 0, HALF, at(1, 0, 0))
        across["near"].append(send(at(3, 0, 0), k, 0, N, sibling))
        f["m0"].wait_recv()
        f["mm0"] = send(at(1, 0, 0), k, HALF, HALF, at(3, 0, 0))
        across["near"].append(send(at(1, 0, 0), k, 0, N, sibling))

    def relay_second(k):
        f = flows[k]
        f["p1"].wait_recv()
        f["pp1"] = send(at(3, 1, 0), k, 0, HALF, at(1, 0, 0))
        across["middle"].append(send(at(3, 1, 0), k, 0, N, sibling))
        f["m1"].wait_recv()
        f["mm1"] = send(at(1, 1, 0), k, HALF, HALF, at(3, 0, 0))
        across["middle"].append(send(at(1, 1, 0), k, 0, N, sibling))

    def relay_third(k):
        f = flows[k]
        f["pp0"].wait_recv()
        f["mm0"].wait_recv()
        across["middle"].append(send(at(2, 0, 0), k, 0, N, sibling))

    def relay_fourth(k):
        f = flows[k]
        f["pp1"].wait_recv()
        f["mm1"].wait_recv()
        across["last"].append(send(at(2, 1, 0), k, 0, N, sibling))

    def all_here(stage):
        for copy in across[stage]:
            copy.wait_recv()

    def turn(weight, degree, first):
        for pair in range(BLOCKS // 2):
            for n in range(degree):
                tiles[pair, first + n] = jnp.transpose(
                    jnp.concatenate(
                        [weight[2 * pair, n].astype(F32), weight[2 * pair + 1, n].astype(F32)], axis=0
                    )
                ).astype(BF16)

    def build(links, count, degree, first, out):
        def pair_of(pair, carry):
            parts = [tiles[pair, first + n] for n in range(degree)]
            wanted = [
                jnp.where(low[0:1], links[n, 2 * pair], links[n, 2 * pair + 1])
                for n in range(degree)
            ]

            def source_blocks(g, c):
                for i in range(4):
                    r = g * 4 + i
                    terms = [
                        p * jnp.where(w == r, 1.0, 0.0).astype(BF16) for p, w in zip(parts, wanted)
                    ]
                    out[
                        pl.ds(pl.multiple_of(r * BS, BS), BS),
                        pl.ds(pl.multiple_of(pair * 128, 128), 128),
                    ] = functools.reduce(lambda u, v: u + v, terms)
                return c

            return lax.fori_loop(0, count // 4, source_blocks, carry)

        lax.fori_loop(0, BLOCKS // 2, pair_of, 0)

    def build_inverse():
        forth[...] = jnp.zeros_like(forth)
        back[...] = jnp.zeros_like(back)
        gap = jnp.zeros((BS, BS), F32)
        for b in range(BLOCKS):
            quad, place = b // 4, b % 4
            value = inverse_w[b].astype(F32)
            for out, tile in ((forth, jnp.transpose(value)), (back, value)):
                wide = jnp.concatenate([tile, gap] if place % 2 == 0 else [gap, tile], axis=1)
                lane = place // 2 * 128
                out[quad, place * BS : (place + 1) * BS, lane : lane + 128] = wide.astype(BF16)

    def couple_local():
        def part(r, carry):
            rows = pl.ds(pl.multiple_of(r * SUB, SUB), SUB)
            for n in range(4):
                cols = slice(n * 256, (n + 1) * 256)
                total[rows, cols] = total[rows, cols] - jnp.dot(
                    ordered[rows, :], near[:, cols], preferred_element_type=F32
                )
            return carry

        lax.fori_loop(0, ROWS // SUB, part, 0)

    def couple_remote(*chips, rows_of=range(CHUNKS)):
        places = [at(dx, dy, 0) // 2 for dx, dy in chips]

        def part(r, carry):
            rows = pl.ds(pl.multiple_of(r * SUB, SUB), SUB)
            k = r // (CHUNK_ROWS // SUB)
            inner = pl.ds(pl.multiple_of(r % (CHUNK_ROWS // SUB) * SUB, SUB), SUB)
            for n in range(4):
                cols = slice(n * 256, (n + 1) * 256)
                left = jnp.concatenate(
                    [shared[k, 2 * q + c, inner, :] for q in places for c in range(2)], axis=1
                )
                right = jnp.concatenate(
                    [far[pl.ds(pl.multiple_of(q * 256, 256), 256), cols] for q in places], axis=0
                )
                total[rows, cols] = total[rows, cols] - jnp.dot(
                    left, right, preferred_element_type=F32
                )
            return carry

        steps = CHUNK_ROWS // SUB
        lax.fori_loop(rows_of[0] * steps, (rows_of[-1] + 1) * steps, part, 0)

    def force(k):
        def part(r, carry):
            rows = pl.ds(pl.multiple_of(r * SUB, SUB), SUB)
            for n in range(4):
                cols = slice(n * 256, (n + 1) * 256)
                states[rows, cols] = jnp.dot(
                    total[rows, cols].astype(BF16), forth[n], preferred_element_type=F32
                )
            return carry

        lax.fori_loop(k * (CHUNK_ROWS // SUB), (k + 1) * (CHUNK_ROWS // SUB), part, 0)

    def scan_forward(k, state):
        def day(t, s):
            s = s * retain[pl.ds(t, 1), :] + states[day_rows(t), :] * active[pl.ds(t, 1), :]
            states[day_rows(t), :] = s
            return s

        return lax.fori_loop(k * CHUNK_DAYS, (k + 1) * CHUNK_DAYS, day, state)

    def prepare_decay():
        on = lax.broadcasted_iota(jnp.int32, (DAYS, WIDTH), 0) < slab_days[0]
        active[...] = jnp.where(on, 1.0, 0.0)
        retain[0:DAYS, :] = jnp.where(on, retention_ref[...], 1.0)
        retain[DAYS : DAYS + 8, :] = jnp.ones((8, WIDTH), F32)

        def ahead(t, d):
            d = d * retain[pl.ds(t, 1), :]
            forward_decay[pl.ds(t, 1), :] = d
            return d

        product = lax.fori_loop(0, DAYS, ahead, jnp.ones((1, WIDTH), F32))

        def behind(i, d):
            t = DAYS - 1 - i
            d = d * retain[pl.ds(t + 1, 1), :]
            backward_decay[pl.ds(t, 1), :] = d
            return d

        lax.fori_loop(0, DAYS, behind, jnp.ones((1, WIDTH), F32))
        for q in range(8):
            slab_decay[tm, q : q + 1, :] = product[:, q * 128 : (q + 1) * 128]

    def tm_copy(buf, to, send, recv):
        return pltpu.make_async_remote_copy(
            src_ref=buf.at[tm],
            dst_ref=buf.at[tm],
            send_sem=tm_send.at[send],
            recv_sem=tm_recv.at[recv],
            device_id=(to, space),
            device_id_type=MESH,
        )

    def exchange(kind, buf, act):
        for d in reversed(range(1, SLABS)):
            ahead = (kind == 1) == (act != "wait_recv")
            other = tm + d if ahead else tm - d
            real = other < SLABS if ahead else other >= 0
            peer = (other + SLABS) % SLABS
            signal = peer if act == "wait_recv" else tm

            @pl.when(real)
            def _():
                getattr(tm_copy(buf, peer, peer, signal), act)()

    def prepare_response():
        for n in range(4):
            cols = slice(n * 256, (n + 1) * 256)
            decay = forward_decay[:, cols]
            gram = lax.dot_general(
                decay * active[:, cols],
                decay,
                (((0,), (0,)), ((), ())),
                precision=lax.Precision.HIGHEST,
                preferred_element_type=F32,
            )
            response[n] = gram * back[n].astype(F32)

    def decay_of(s):
        return jnp.concatenate([slab_decay[s, q : q + 1, :] for q in range(8)], axis=1)

    for k in range(CHUNKS):
        fetch[k].wait()
    pick_shared()
    for copy in weights:
        copy.start()
    pl.semaphore_wait(barrier, 4 + SLABS - 1)
    for k in range(CHUNKS):
        send_own(k)
    prepare_decay()
    decay_copies = [
        tm_copy(slab_decay, (tm + d) % SLABS, SLABS + d - 1, SLABS + d - 1)
        for d in range(1, SLABS)
    ]
    for copy in decay_copies:
        copy.start()
    permute(0)
    permute(1)
    order(0)
    order(1)
    weights[0].wait()
    weights[1].wait()
    turn(local_w, 4, 0)
    turn(remote_w, 2, 4)
    relay_first(0)
    relay_own_row(0)
    relay_first(1)
    build(local_links, BLOCKS, 4, 0, near)
    build(remote_links, 2 * GROUPS, 2, 4, far)
    relay_own_row(1)
    couple_local()
    relay_second(0)
    relay_second(1)
    all_here("near")
    couple_remote((0, 0), (1, 0), (3, 0), (0, 1))
    relay_third(0)
    relay_third(1)
    weights[2].wait()
    build_inverse()
    prepare_response()
    all_here("middle")
    couple_remote((2, 0), (1, 1), (3, 1))
    relay_fourth(0)
    relay_fourth(1)
    state = jnp.zeros((PROBES, WIDTH), F32)
    for k in range(CHUNKS):
        across["last"][k].wait_recv()
        couple_remote((2, 1), rows_of=[k])
        force(k)
        state = scan_forward(k, state)
    ends[tm] = state.astype(BF16)
    exchange(1, ends, "start")

    row8 = lax.broadcasted_iota(jnp.int32, (8, 128), 0)

    def fold(values):
        for step in (1, 2, 4):
            keep = (row8 & step) == 0
            values = [
                jnp.where(keep, u, v) + pltpu.roll(jnp.where(keep, v, u), step, 0)
                for u, v in zip(values[0::2], values[1::2])
            ]
        return values[0]

    def adjoint_sweep(carry, with_sums):
        def fix(g, c):
            for i in range(2):
                t = 2 * g + i
                value = states[day_rows(t), :]
                if with_sums:
                    value = value + forward_decay[pl.ds(t, 1), :] * c
                stored[day_rows(t), :] = value.astype(BF16)
            return c

        lax.fori_loop(0, DAYS // 2, fix, carry)

        def part(r, c):
            rows = pl.ds(pl.multiple_of(r * SUB, SUB), SUB)
            for n in range(4):
                cols = slice(n * 256, (n + 1) * 256)
                total[rows, cols] = jnp.dot(stored[rows, cols], back[n], preferred_element_type=F32)
            return c

        lax.fori_loop(0, ROWS // SUB, part, 0)
        leave = []
        for n in range(4):
            cols = slice(n * 256, (n + 1) * 256)

            def days(i, u):
                g = DAYS // 8 - 1 - i
                sums = [[None] * 8, [None] * 8]
                for j in reversed(range(8)):
                    t = g * 8 + j
                    u = total[day_rows(t), cols] * active[pl.ds(t, 1), cols] + retain[
                        pl.ds(t + 1, 1), cols
                    ] * u
                    if with_sums:
                        product = ordered[day_rows(t), cols].astype(F32) * u
                        for h in range(2):
                            half = product[:, h * 128 : (h + 1) * 128]
                            sums[h][j] = half[0:8] + half[8:16]
                if with_sums:
                    eight = pl.ds(pl.multiple_of(g * 8, 8), 8)
                    for h in range(2):
                        lane = n * 256 + h * 128
                        partial[eight, lane : lane + 128] = fold(sums[h])
                return u

            leave.append(
                lax.fori_loop(0, DAYS // 8, days, jnp.zeros((PROBES, 256), F32))
                * retain[0:1, cols]
            )
        return leave

    leave = adjoint_sweep(0, False)
    for copy in decay_copies:
        copy.wait_recv()
    exchange(1, ends, "wait_recv")
    carry = jnp.zeros((PROBES, WIDTH), F32)
    for s in range(SLABS - 1):
        carry = jnp.where(s < tm, decay_of(s) * carry + ends[s].astype(F32), carry)
    for n in range(4):
        cols = slice(n * 256, (n + 1) * 256)
        value = leave[n] + jnp.dot(
            carry[:, cols],
            response[n],
            precision=lax.Precision.HIGHEST,
            preferred_element_type=F32,
        )
        leaving[tm, :, cols] = value.astype(BF16)
    exchange(2, leaving, "start")
    adjoint_sweep(carry, True)

    for copy in pending:
        copy.wait_send()
    for copy in decay_copies:
        copy.wait_send()
    exchange(1, ends, "wait_send")
    exchange(2, leaving, "wait_recv")

    carry = jnp.zeros((PROBES, WIDTH), F32)
    for s in reversed(range(1, SLABS)):
        carry = jnp.where(s > tm, decay_of(s) * carry + leaving[s].astype(F32), carry)

    def finish(g, c):
        eight = pl.ds(pl.multiple_of(g * 8, 8), 8)
        for n in range(8):
            cols = slice(n * 128, (n + 1) * 128)
            top, bottom = c[0:8, cols], c[8:16, cols]
            z = ordered[pl.ds(pl.multiple_of(g * 128, 128), 128), cols].astype(F32)
            extra = fold(
                [
                    z[16 * d : 16 * d + 8] * top + z[16 * d + 8 : 16 * d + 16] * bottom
                    for d in range(8)
                ]
            )
            out_ref[eight, cols] = (partial[eight, cols] + backward_decay[eight, cols] * extra) * (
                1.0 / PROBES
            )
        return c

    lax.fori_loop(0, DAYS // 8, finish, carry)
    exchange(2, leaving, "wait_send")


def local(
    probes,
    local_links,
    remote_links,
    shared_blocks,
    slab_days,
    local_coupling,
    remote_coupling,
    block_inverse,
    retention,
):
    smem = pl.BlockSpec(memory_space=pltpu.SMEM)
    vmem = pl.BlockSpec(memory_space=pltpu.VMEM)
    anywhere = pl.BlockSpec(memory_space=pl.ANY)
    return pl.pallas_call(
        kernel,
        out_shape=jax.ShapeDtypeStruct((DAYS, WIDTH), F32),
        in_specs=[smem] * 4 + [anywhere] * 4 + [vmem],
        out_specs=vmem,
        scratch_shapes=[
            pltpu.VMEM((ROWS, WIDTH), BF16),
            pltpu.VMEM(local_coupling.shape, BF16),
            pltpu.VMEM(remote_coupling.shape, BF16),
            pltpu.VMEM(block_inverse.shape, BF16),
            pltpu.VMEM((WIDTH, WIDTH), BF16),
            pltpu.VMEM((ROWS * 8, 128), F32),
            pltpu.VMEM((2 * DAYS, WIDTH), BF16),
            pltpu.VMEM((2 * DAYS * 8, 128), F32),
            pltpu.VMEM((ROWS, WIDTH), BF16),
            pltpu.VMEM((CHUNKS, GROUPS, CHUNK_ROWS, 128), BF16),
            pltpu.VMEM((BLOCKS // 2, 6, BS, 128), BF16),
            pltpu.VMEM((WIDTH, WIDTH), BF16),
            pltpu.VMEM((2 * WIDTH, WIDTH), BF16),
            pltpu.VMEM((4, 256, 256), BF16),
            pltpu.VMEM((4, 256, 256), BF16),
            pltpu.VMEM((ROWS, WIDTH), F32),
            pltpu.VMEM((ROWS, WIDTH), F32),
            pltpu.VMEM((ROWS, WIDTH), BF16),
            pltpu.VMEM((DAYS + 8, WIDTH), F32),
            pltpu.VMEM((DAYS, WIDTH), F32),
            pltpu.VMEM((DAYS, WIDTH), F32),
            pltpu.VMEM((DAYS, WIDTH), F32),
            pltpu.VMEM((DAYS, WIDTH), F32),
            pltpu.VMEM((SLABS, 8, 128), F32),
            pltpu.VMEM((4, 256, 256), F32),
            pltpu.VMEM((SLABS, PROBES, WIDTH), BF16),
            pltpu.VMEM((SLABS, PROBES, WIDTH), BF16),
            pltpu.SemaphoreType.DMA((CHUNKS + 3,)),
            pltpu.SemaphoreType.DMA((CHUNKS * 17,)),
            pltpu.SemaphoreType.DMA((CHUNKS * 17,)),
            pltpu.SemaphoreType.DMA((2 * SLABS - 1,)),
            pltpu.SemaphoreType.DMA((2 * SLABS - 1,)),
        ],
        compiler_params=pltpu.CompilerParams(
            vmem_limit_bytes=60 << 20, collective_id=0, has_side_effects=True
        ),
    )(
        local_links.T,
        remote_links.T,
        shared_blocks,
        slab_days,
        probes.reshape(ROWS, WIDTH),
        local_coupling,
        remote_coupling,
        block_inverse,
        retention,
    )


def solution(mesh):
    placed = (
        P("tm", "space", None),
        P("space", None),
        P("space", None),
        P("space", None),
        P("tm"),
        P("space", None, None, None),
        P("space", None, None, None),
        P("space", None, None),
        P("tm", "space"),
    )
    return jax.shard_map(
        local, mesh=mesh, in_specs=placed, out_specs=P("tm", "space"), check_vma=False
    )
```

```python
import functools

import jax
import jax.numpy as jnp
from jax import lax
from jax.experimental import pallas as pl
from jax.experimental.pallas import tpu as pltpu
from jax.sharding import PartitionSpec as P

F32, BF16 = jnp.float32, jnp.bfloat16
MESH = pl.DeviceIdType.MESH
DAYS, BLOCKS, BS, PROBES, GROUPS, SLABS = 48, 16, 64, 16, 16, 8
WIDTH = BLOCKS * BS
ROWS = DAYS * PROBES
CHUNKS = 2
CHUNK_ROWS = ROWS // CHUNKS
CHUNK_DAYS = DAYS // CHUNKS
HALF = CHUNK_ROWS // 2
SUB = 192


def day_rows(t):
    return pl.ds(pl.multiple_of(t * PROBES, PROBES), PROBES)


def kernel(
    local_links,
    remote_links,
    shared_blocks,
    slab_days,
    probes_hbm,
    local_hbm,
    remote_hbm,
    inverse_hbm,
    retention_ref,
    out_ref,
    probes,
    local_w,
    remote_w,
    inverse_w,
    shuffle,
    shuffled,
    picked,
    picked_shuffled,
    ordered,
    shared,
    tiles,
    near,
    far,
    forth,
    back,
    total,
    states,
    stored,
    retain,
    active,
    forward_decay,
    backward_decay,
    partial,
    slab_decay,
    response,
    ends,
    leaving,
    in_sem,
    send_sem,
    recv_sem,
    tm_send,
    tm_recv,
):
    tm = lax.axis_index("tm")
    space = lax.axis_index("space")
    core, x, y = space % 2, (space // 2) % 4, space // 8

    def at(dx, dy, dc):
        return ((y + dy) % 2 * 4 + (x + dx) % 4) * 2 + (core + dc) % 2

    me = at(0, 0, 0)
    sibling = at(0, 0, 1)

    barrier = pltpu.get_barrier_semaphore()
    for to in (at(1, 0, 0), at(3, 0, 0), at(0, 1, 0), sibling):
        pl.semaphore_signal(barrier, inc=1, device_id=(tm, to), device_id_type=MESH)
    for d in range(1, SLABS):
        pl.semaphore_signal(
            barrier, inc=1, device_id=((tm + d) % SLABS, space), device_id_type=MESH
        )

    fetch = []
    for k in range(CHUNKS):
        rows = pl.ds(k * CHUNK_ROWS, CHUNK_ROWS)
        fetch.append(pltpu.make_async_copy(probes_hbm.at[rows], probes.at[rows], in_sem.at[k]))
    weights = [
        pltpu.make_async_copy(local_hbm, local_w, in_sem.at[CHUNKS]),
        pltpu.make_async_copy(remote_hbm, remote_w, in_sem.at[CHUNKS + 1]),
        pltpu.make_async_copy(inverse_hbm, inverse_w, in_sem.at[CHUNKS + 2]),
    ]
    for copy in fetch:
        copy.start()

    def shuffle_rows(r, carry):
        source = lax.broadcasted_iota(jnp.int32, (64, 128), 0) + r * 64
        gap = (source & (PROBES - 1)) * BS + (source >> 4)
        gap = gap - lax.broadcasted_iota(jnp.int32, (64, 128), 1)
        for q in range(8):
            shuffle[pl.ds(pl.multiple_of(r * 64, 64), 64), q * 128 : (q + 1) * 128] = jnp.where(
                gap == q * 128, 1.0, 0.0
            ).astype(BF16)
        return carry

    lax.fori_loop(0, WIDTH // 64, shuffle_rows, 0)

    low = lax.broadcasted_iota(jnp.int32, (8, 128), 1) < BS

    def pair_up(first, second):
        mixed = pltpu.roll(jnp.where(low, second, first), BS, 1)
        return jnp.concatenate(
            [jnp.where(low, first, mixed), jnp.where(low, mixed, second)], axis=0
        )

    def block_row(t, b):
        return shuffled[pl.ds(pl.multiple_of((t * BLOCKS + b) * 8, 8), 8), :]

    def permute(k):
        def part(r, carry):
            lo = k * CHUNK_ROWS + r * SUB
            for n in range(4):
                value = jnp.dot(
                    probes[pl.ds(pl.multiple_of(lo, SUB), SUB), :],
                    shuffle[:, n * 256 : (n + 1) * 256],
                    preferred_element_type=F32,
                )
                for h in range(2):
                    shuffled[pl.ds(lo * 8 + 2 * n + h, SUB, stride=8), :] = value[
                        :, h * 128 : (h + 1) * 128
                    ]
            return carry

        lax.fori_loop(0, CHUNK_ROWS // SUB, part, 0)

    def pick_shared():
        row = lax.broadcasted_iota(jnp.int32, (2 * DAYS, ROWS), 0)
        column = lax.broadcasted_iota(jnp.int32, (2 * DAYS, ROWS), 1)
        second = row >= DAYS
        day = jnp.where(second, row - DAYS, row)
        wanted = day * BLOCKS + jnp.where(second, shared_blocks[0, 1], shared_blocks[0, 0])
        select = jnp.where(column == wanted, 1.0, 0.0).astype(BF16)
        for n in range(4):
            cols = slice(n * 256, (n + 1) * 256)
            picked[:, cols] = jnp.dot(
                select, probes[:, cols], preferred_element_type=F32
            ).astype(BF16)
        for n in range(4):
            value = jnp.dot(
                picked[...], shuffle[:, n * 256 : (n + 1) * 256], preferred_element_type=F32
            )
            for h in range(2):
                picked_shuffled[pl.ds(2 * n + h, 2 * DAYS, stride=8), :] = value[
                    :, h * 128 : (h + 1) * 128
                ]

        def days(g, carry):
            for i in range(4):
                t = g * 4 + i
                tiles = [
                    picked_shuffled[pl.ds(pl.multiple_of((m * DAYS + t) * 8, 8), 8), :]
                    for m in range(2)
                ]
                shared[t // CHUNK_DAYS, me, day_rows(t % CHUNK_DAYS), :] = pair_up(*tiles).astype(BF16)
            return carry

        lax.fori_loop(0, DAYS // 4, days, 0)

    def order(k):
        def days(g, carry):
            for i in range(4):
                t = g * 4 + i
                for pair in range(BLOCKS // 2):
                    value = pair_up(block_row(t, 2 * pair), block_row(t, 2 * pair + 1))
                    total[day_rows(t), pair * 128 : (pair + 1) * 128] = value
                    ordered[day_rows(t), pair * 128 : (pair + 1) * 128] = value.astype(BF16)
            return carry

        lax.fori_loop(k * CHUNK_DAYS // 4, (k + 1) * CHUNK_DAYS // 4, days, 0)

    used = [0]
    pending = []

    def send(slot, k, lo, rows, to):
        i = used[0]
        used[0] += 1
        where = shared.at[k, slot, pl.ds(lo, rows)]
        copy = pltpu.make_async_remote_copy(
            src_ref=where,
            dst_ref=where,
            send_sem=send_sem.at[i],
            recv_sem=recv_sem.at[i],
            device_id=(tm, to),
            device_id_type=MESH,
        )
        copy.start()
        pending.append(copy)
        return copy

    flows = [{} for _ in range(CHUNKS)]
    across = {"near": [], "middle": [], "last": []}
    N = CHUNK_ROWS

    def send_own(k):
        f = flows[k]
        f["y"] = send(me, k, 0, N, at(0, 1, 0))
        f["p0"] = send(me, k, 0, N, at(1, 0, 0))
        f["m0"] = send(me, k, 0, N, at(3, 0, 0))
        across["near"].append(send(me, k, 0, N, sibling))

    def relay_first(k):
        f = flows[k]
        f["y"].wait_recv()
        f["p1"] = send(at(0, 1, 0), k, 0, HALF, at(1, 0, 0))
        f["m1"] = send(at(0, 1, 0), k, HALF, HALF, at(3, 0, 0))
        across["near"].append(send(at(0, 1, 0), k, 0, N, sibling))

    def relay_own_row(k):
        f = flows[k]
        f["p0"].wait_recv()
        f["pp0"] = send(at(3, 0, 0), k, 0, HALF, at(1, 0, 0))
        f["yp"] = send(at(3, 0, 0), k, HALF, HALF, at(0, 1, 0))
        across["near"].append(send(at(3, 0, 0), k, 0, N, sibling))
        f["m0"].wait_recv()
        f["mm0"] = send(at(1, 0, 0), k, HALF, HALF, at(3, 0, 0))
        f["ym"] = send(at(1, 0, 0), k, 0, HALF, at(0, 1, 0))
        across["near"].append(send(at(1, 0, 0), k, 0, N, sibling))

    def relay_second(k):
        f = flows[k]
        f["p1"].wait_recv()
        f["pp1"] = send(at(3, 1, 0), k, 0, HALF, at(1, 0, 0))
        f["m1"].wait_recv()
        f["mm1"] = send(at(1, 1, 0), k, HALF, HALF, at(3, 0, 0))

    def relay_third(k):
        f = flows[k]
        f["pp0"].wait_recv()
        f["mm0"].wait_recv()
        across["middle"].append(send(at(2, 0, 0), k, 0, N, sibling))
        f["yp"].wait_recv()
        across["middle"].append(send(at(3, 1, 0), k, 0, N, sibling))
        f["ym"].wait_recv()
        across["middle"].append(send(at(1, 1, 0), k, 0, N, sibling))

    def relay_fourth(k):
        f = flows[k]
        f["pp1"].wait_recv()
        f["mm1"].wait_recv()
        across["last"].append(send(at(2, 1, 0), k, 0, N, sibling))

    def all_here(stage):
        for copy in across[stage]:
            copy.wait_recv()

    def turn(weight, degree, first):
        for pair in range(BLOCKS // 2):
            for n in range(degree):
                tiles[pair, first + n] = jnp.transpose(
                    jnp.concatenate(
                        [weight[2 * pair, n].astype(F32), weight[2 * pair + 1, n].astype(F32)], axis=0
                    )
                ).astype(BF16)

    def build(links, count, degree, first, out):
        def pair_of(pair, carry):
            parts = [tiles[pair, first + n] for n in range(degree)]
            wanted = [
                jnp.where(low[0:1], links[n, 2 * pair], links[n, 2 * pair + 1])
                for n in range(degree)
            ]

            def source_blocks(g, c):
                for i in range(4):
                    r = g * 4 + i
                    terms = [
                        p * jnp.where(w == r, 1.0, 0.0).astype(BF16) for p, w in zip(parts, wanted)
                    ]
                    out[
                        pl.ds(pl.multiple_of(r * BS, BS), BS),
                        pl.ds(pl.multiple_of(pair * 128, 128), 128),
                    ] = functools.reduce(lambda u, v: u + v, terms)
                return c

            return lax.fori_loop(0, count // 4, source_blocks, carry)

        lax.fori_loop(0, BLOCKS // 2, pair_of, 0)

    def build_inverse():
        forth[...] = jnp.zeros_like(forth)
        back[...] = jnp.zeros_like(back)
        gap = jnp.zeros((BS, BS), F32)
        for b in range(BLOCKS):
            quad, place = b // 4, b % 4
            value = inverse_w[b].astype(F32)
            for out, tile in ((forth, jnp.transpose(value)), (back, value)):
                wide = jnp.concatenate([tile, gap] if place % 2 == 0 else [gap, tile], axis=1)
                lane = place // 2 * 128
                out[quad, place * BS : (place + 1) * BS, lane : lane + 128] = wide.astype(BF16)

    def couple_local(k):
        def part(r, carry):
            rows = pl.ds(pl.multiple_of(r * SUB, SUB), SUB)
            for n in range(4):
                cols = slice(n * 256, (n + 1) * 256)
                total[rows, cols] = total[rows, cols] - jnp.dot(
                    ordered[rows, :], near[:, cols], preferred_element_type=F32
                )
            return carry

        lax.fori_loop(k * (CHUNK_ROWS // SUB), (k + 1) * (CHUNK_ROWS // SUB), part, 0)

    def couple_remote(*chips, rows_of=range(CHUNKS)):
        places = [at(dx, dy, 0) // 2 for dx, dy in chips]

        def part(r, carry):
            rows = pl.ds(pl.multiple_of(r * SUB, SUB), SUB)
            k = r // (CHUNK_ROWS // SUB)
            inner = pl.ds(pl.multiple_of(r % (CHUNK_ROWS // SUB) * SUB, SUB), SUB)
            for n in range(4):
                cols = slice(n * 256, (n + 1) * 256)
                left = jnp.concatenate(
                    [shared[k, 2 * q + c, inner, :] for q in places for c in range(2)], axis=1
                )
                right = jnp.concatenate(
                    [far[pl.ds(pl.multiple_of(q * 256, 256), 256), cols] for q in places], axis=0
                )
                total[rows, cols] = total[rows, cols] - jnp.dot(
                    left, right, preferred_element_type=F32
                )
            return carry

        steps = CHUNK_ROWS // SUB
        lax.fori_loop(rows_of[0] * steps, (rows_of[-1] + 1) * steps, part, 0)

    def force(k):
        def part(r, carry):
            rows = pl.ds(pl.multiple_of(r * SUB, SUB), SUB)
            for n in range(4):
                cols = slice(n * 256, (n + 1) * 256)
                states[rows, cols] = jnp.dot(
                    total[rows, cols].astype(BF16), forth[n], preferred_element_type=F32
                )
            return carry

        lax.fori_loop(k * (CHUNK_ROWS // SUB), (k + 1) * (CHUNK_ROWS // SUB), part, 0)

    def scan_forward(k, state):
        def day(t, s):
            s = s * retain[pl.ds(t, 1), :] + states[day_rows(t), :] * active[pl.ds(t, 1), :]
            states[day_rows(t), :] = s
            return s

        return lax.fori_loop(k * CHUNK_DAYS, (k + 1) * CHUNK_DAYS, day, state)

    def prepare_decay():
        on = lax.broadcasted_iota(jnp.int32, (DAYS, WIDTH), 0) < slab_days[0]
        active[...] = jnp.where(on, 1.0, 0.0)
        retain[0:DAYS, :] = jnp.where(on, retention_ref[...], 1.0)
        retain[DAYS : DAYS + 8, :] = jnp.ones((8, WIDTH), F32)

        def ahead(t, d):
            d = d * retain[pl.ds(t, 1), :]
            forward_decay[pl.ds(t, 1), :] = d
            return d

        product = lax.fori_loop(0, DAYS, ahead, jnp.ones((1, WIDTH), F32))

        def behind(i, d):
            t = DAYS - 1 - i
            d = d * retain[pl.ds(t + 1, 1), :]
            backward_decay[pl.ds(t, 1), :] = d
            return d

        lax.fori_loop(0, DAYS, behind, jnp.ones((1, WIDTH), F32))
        for q in range(8):
            slab_decay[tm, q : q + 1, :] = product[:, q * 128 : (q + 1) * 128]

    def tm_copy(buf, to, send, recv):
        return pltpu.make_async_remote_copy(
            src_ref=buf.at[tm],
            dst_ref=buf.at[tm],
            send_sem=tm_send.at[send],
            recv_sem=tm_recv.at[recv],
            device_id=(to, space),
            device_id_type=MESH,
        )

    def exchange(kind, buf, act):
        for d in reversed(range(1, SLABS)):
            ahead = (kind == 1) == (act != "wait_recv")
            other = tm + d if ahead else tm - d
            real = other < SLABS if ahead else other >= 0
            peer = (other + SLABS) % SLABS
            signal = peer if act == "wait_recv" else tm

            @pl.when(real)
            def _():
                getattr(tm_copy(buf, peer, peer, signal), act)()

    def prepare_response():
        for n in range(4):
            cols = slice(n * 256, (n + 1) * 256)
            decay = forward_decay[:, cols]
            gram = lax.dot_general(
                decay * active[:, cols],
                decay,
                (((0,), (0,)), ((), ())),
                precision=lax.Precision.HIGHEST,
                preferred_element_type=F32,
            )
            response[n] = gram * back[n].astype(F32)

    def decay_of(s):
        return jnp.concatenate([slab_decay[s, q : q + 1, :] for q in range(8)], axis=1)

    for k in range(CHUNKS):
        fetch[k].wait()
    pick_shared()
    for copy in weights:
        copy.start()
    pl.semaphore_wait(barrier, 4 + SLABS - 1)
    for k in range(CHUNKS):
        send_own(k)
    prepare_decay()
    decay_copies = [
        tm_copy(slab_decay, (tm + d) % SLABS, SLABS + d - 1, SLABS + d - 1)
        for d in range(1, SLABS)
    ]
    for copy in decay_copies:
        copy.start()
    permute(0)
    permute(1)
    order(0)
    order(1)
    weights[0].wait()
    weights[1].wait()
    turn(local_w, 4, 0)
    turn(remote_w, 2, 4)
    relay_first(0)
    relay_own_row(0)
    relay_first(1)
    relay_own_row(1)
    build(local_links, BLOCKS, 4, 0, near)
    build(remote_links, 2 * GROUPS, 2, 4, far)
    couple_local(0)
    relay_second(0)
    couple_local(1)
    relay_second(1)
    all_here("near")
    couple_remote((0, 0), (1, 0), (3, 0), (0, 1))
    relay_third(0)
    relay_third(1)
    weights[2].wait()
    build_inverse()
    prepare_response()
    all_here("middle")
    couple_remote((2, 0), (1, 1), (3, 1))
    relay_fourth(0)
    relay_fourth(1)
    state = jnp.zeros((PROBES, WIDTH), F32)
    for k in range(CHUNKS):
        across["last"][k].wait_recv()
        couple_remote((2, 1), rows_of=[k])
        force(k)
        state = scan_forward(k, state)
    ends[tm] = state.astype(BF16)
    exchange(1, ends, "start")

    row8 = lax.broadcasted_iota(jnp.int32, (8, 128), 0)

    def fold(values):
        for step in (1, 2, 4):
            keep = (row8 & step) == 0
            values = [
                jnp.where(keep, u, v) + pltpu.roll(jnp.where(keep, v, u), step, 0)
                for u, v in zip(values[0::2], values[1::2])
            ]
        return values[0]

    def adjoint_sweep(carry, with_sums):
        def fix(g, c):
            for i in range(2):
                t = 2 * g + i
                value = states[day_rows(t), :]
                if with_sums:
                    value = value + forward_decay[pl.ds(t, 1), :] * c
                stored[day_rows(t), :] = value.astype(BF16)
            return c

        lax.fori_loop(0, DAYS // 2, fix, carry)

        def part(r, c):
            rows = pl.ds(pl.multiple_of(r * SUB, SUB), SUB)
            for n in range(4):
                cols = slice(n * 256, (n + 1) * 256)
                total[rows, cols] = jnp.dot(stored[rows, cols], back[n], preferred_element_type=F32)
            return c

        lax.fori_loop(0, ROWS // SUB, part, 0)
        leave = []
        for n in range(4):
            cols = slice(n * 256, (n + 1) * 256)

            def days(i, u):
                g = DAYS // 8 - 1 - i
                sums = [[None] * 8, [None] * 8]
                for j in reversed(range(8)):
                    t = g * 8 + j
                    u = total[day_rows(t), cols] * active[pl.ds(t, 1), cols] + retain[
                        pl.ds(t + 1, 1), cols
                    ] * u
                    if with_sums:
                        product = ordered[day_rows(t), cols].astype(F32) * u
                        for h in range(2):
                            half = product[:, h * 128 : (h + 1) * 128]
                            sums[h][j] = half[0:8] + half[8:16]
                if with_sums:
                    eight = pl.ds(pl.multiple_of(g * 8, 8), 8)
                    for h in range(2):
                        lane = n * 256 + h * 128
                        partial[eight, lane : lane + 128] = fold(sums[h])
                return u

            leave.append(
                lax.fori_loop(0, DAYS // 8, days, jnp.zeros((PROBES, 256), F32))
                * retain[0:1, cols]
            )
        return leave

    leave = adjoint_sweep(0, False)
    for copy in decay_copies:
        copy.wait_recv()
    exchange(1, ends, "wait_recv")
    carry = jnp.zeros((PROBES, WIDTH), F32)
    for s in range(SLABS - 1):
        carry = jnp.where(s < tm, decay_of(s) * carry + ends[s].astype(F32), carry)
    for n in range(4):
        cols = slice(n * 256, (n + 1) * 256)
        value = leave[n] + jnp.dot(
            carry[:, cols],
            response[n],
            precision=lax.Precision.HIGHEST,
            preferred_element_type=F32,
        )
        leaving[tm, :, cols] = value.astype(BF16)
    exchange(2, leaving, "start")
    adjoint_sweep(carry, True)

    for copy in pending:
        copy.wait_send()
    for copy in decay_copies:
        copy.wait_send()
    exchange(1, ends, "wait_send")
    exchange(2, leaving, "wait_recv")

    carry = jnp.zeros((PROBES, WIDTH), F32)
    for s in reversed(range(1, SLABS)):
        carry = jnp.where(s > tm, decay_of(s) * carry + leaving[s].astype(F32), carry)

    def finish(g, c):
        eight = pl.ds(pl.multiple_of(g * 8, 8), 8)
        for n in range(8):
            cols = slice(n * 128, (n + 1) * 128)
            top, bottom = c[0:8, cols], c[8:16, cols]
            z = ordered[pl.ds(pl.multiple_of(g * 128, 128), 128), cols].astype(F32)
            extra = fold(
                [
                    z[16 * d : 16 * d + 8] * top + z[16 * d + 8 : 16 * d + 16] * bottom
                    for d in range(8)
                ]
            )
            out_ref[eight, cols] = (partial[eight, cols] + backward_decay[eight, cols] * extra) * (
                1.0 / PROBES
            )
        return c

    lax.fori_loop(0, DAYS // 8, finish, carry)
    exchange(2, leaving, "wait_send")


def local(
    probes,
    local_links,
    remote_links,
    shared_blocks,
    slab_days,
    local_coupling,
    remote_coupling,
    block_inverse,
    retention,
):
    smem = pl.BlockSpec(memory_space=pltpu.SMEM)
    vmem = pl.BlockSpec(memory_space=pltpu.VMEM)
    anywhere = pl.BlockSpec(memory_space=pl.ANY)
    return pl.pallas_call(
        kernel,
        out_shape=jax.ShapeDtypeStruct((DAYS, WIDTH), F32),
        in_specs=[smem] * 4 + [anywhere] * 4 + [vmem],
        out_specs=vmem,
        scratch_shapes=[
            pltpu.VMEM((ROWS, WIDTH), BF16),
            pltpu.VMEM(local_coupling.shape, BF16),
            pltpu.VMEM(remote_coupling.shape, BF16),
            pltpu.VMEM(block_inverse.shape, BF16),
            pltpu.VMEM((WIDTH, WIDTH), BF16),
            pltpu.VMEM((ROWS * 8, 128), F32),
            pltpu.VMEM((2 * DAYS, WIDTH), BF16),
            pltpu.VMEM((2 * DAYS * 8, 128), F32),
            pltpu.VMEM((ROWS, WIDTH), BF16),
            pltpu.VMEM((CHUNKS, GROUPS, CHUNK_ROWS, 128), BF16),
            pltpu.VMEM((BLOCKS // 2, 6, BS, 128), BF16),
            pltpu.VMEM((WIDTH, WIDTH), BF16),
            pltpu.VMEM((2 * WIDTH, WIDTH), BF16),
            pltpu.VMEM((4, 256, 256), BF16),
            pltpu.VMEM((4, 256, 256), BF16),
            pltpu.VMEM((ROWS, WIDTH), F32),
            pltpu.VMEM((ROWS, WIDTH), F32),
            pltpu.VMEM((ROWS, WIDTH), BF16),
            pltpu.VMEM((DAYS + 8, WIDTH), F32),
            pltpu.VMEM((DAYS, WIDTH), F32),
            pltpu.VMEM((DAYS, WIDTH), F32),
            pltpu.VMEM((DAYS, WIDTH), F32),
            pltpu.VMEM((DAYS, WIDTH), F32),
            pltpu.VMEM((SLABS, 8, 128), F32),
            pltpu.VMEM((4, 256, 256), F32),
            pltpu.VMEM((SLABS, PROBES, WIDTH), BF16),
            pltpu.VMEM((SLABS, PROBES, WIDTH), BF16),
            pltpu.SemaphoreType.DMA((CHUNKS + 3,)),
            pltpu.SemaphoreType.DMA((CHUNKS * 19,)),
            pltpu.SemaphoreType.DMA((CHUNKS * 19,)),
            pltpu.SemaphoreType.DMA((2 * SLABS - 1,)),
            pltpu.SemaphoreType.DMA((2 * SLABS - 1,)),
        ],
        compiler_params=pltpu.CompilerParams(
            vmem_limit_bytes=60 << 20, collective_id=0, has_side_effects=True
        ),
    )(
        local_links.T,
        remote_links.T,
        shared_blocks,
        slab_days,
        probes.reshape(ROWS, WIDTH),
        local_coupling,
        remote_coupling,
        block_inverse,
        retention,
    )


def solution(mesh):
    placed = (
        P("tm", "space", None),
        P("space", None),
        P("space", None),
        P("space", None),
        P("tm"),
        P("space", None, None, None),
        P("space", None, None, None),
        P("space", None, None),
        P("tm", "space"),
    )
    return jax.shard_map(
        local, mesh=mesh, in_specs=placed, out_specs=P("tm", "space"), check_vma=False
    )
```

```python
import functools

import jax
import jax.numpy as jnp
from jax import lax
from jax.experimental import pallas as pl
from jax.experimental.pallas import tpu as pltpu
from jax.sharding import PartitionSpec as P

F32, BF16 = jnp.float32, jnp.bfloat16
MESH = pl.DeviceIdType.MESH
DAYS, BLOCKS, BS, PROBES, GROUPS, SLABS = 48, 16, 64, 16, 16, 8
WIDTH = BLOCKS * BS
ROWS = DAYS * PROBES
CHUNKS = 2
CHUNK_ROWS = ROWS // CHUNKS
CHUNK_DAYS = DAYS // CHUNKS
HALF = CHUNK_ROWS // 2
SUB = 192


def day_rows(t):
    return pl.ds(pl.multiple_of(t * PROBES, PROBES), PROBES)


def kernel(
    local_links,
    remote_links,
    shared_blocks,
    slab_days,
    probes_hbm,
    local_hbm,
    remote_hbm,
    inverse_hbm,
    retention_ref,
    out_ref,
    probes,
    local_w,
    remote_w,
    inverse_w,
    shuffle,
    shuffled,
    picked,
    picked_shuffled,
    ordered,
    shared,
    tiles,
    near,
    far,
    forth,
    back,
    total,
    states,
    stored,
    retain,
    active,
    forward_decay,
    backward_decay,
    partial,
    slab_decay,
    response,
    ends,
    leaving,
    in_sem,
    send_sem,
    recv_sem,
    tm_send,
    tm_recv,
):
    tm = lax.axis_index("tm")
    space = lax.axis_index("space")
    core, x, y = space % 2, (space // 2) % 4, space // 8

    def at(dx, dy, dc):
        return ((y + dy) % 2 * 4 + (x + dx) % 4) * 2 + (core + dc) % 2

    me = at(0, 0, 0)
    sibling = at(0, 0, 1)

    barrier = pltpu.get_barrier_semaphore()
    for to in (at(1, 0, 0), at(3, 0, 0), at(0, 1, 0), sibling):
        pl.semaphore_signal(barrier, inc=1, device_id=(tm, to), device_id_type=MESH)
    for d in range(1, SLABS):
        pl.semaphore_signal(
            barrier, inc=1, device_id=((tm + d) % SLABS, space), device_id_type=MESH
        )

    fetch = []
    for k in range(CHUNKS):
        rows = pl.ds(k * CHUNK_ROWS, CHUNK_ROWS)
        fetch.append(pltpu.make_async_copy(probes_hbm.at[rows], probes.at[rows], in_sem.at[k]))
    weights = [
        pltpu.make_async_copy(local_hbm, local_w, in_sem.at[CHUNKS]),
        pltpu.make_async_copy(remote_hbm, remote_w, in_sem.at[CHUNKS + 1]),
        pltpu.make_async_copy(inverse_hbm, inverse_w, in_sem.at[CHUNKS + 2]),
    ]
    for copy in fetch:
        copy.start()

    def shuffle_rows(r, carry):
        source = lax.broadcasted_iota(jnp.int32, (64, 128), 0) + r * 64
        gap = (source & (PROBES - 1)) * BS + (source >> 4)
        gap = gap - lax.broadcasted_iota(jnp.int32, (64, 128), 1)
        for q in range(8):
            shuffle[pl.ds(pl.multiple_of(r * 64, 64), 64), q * 128 : (q + 1) * 128] = jnp.where(
                gap == q * 128, 1.0, 0.0
            ).astype(BF16)
        return carry

    lax.fori_loop(0, WIDTH // 64, shuffle_rows, 0)

    low = lax.broadcasted_iota(jnp.int32, (8, 128), 1) < BS

    def pair_up(first, second):
        mixed = pltpu.roll(jnp.where(low, second, first), BS, 1)
        return jnp.concatenate(
            [jnp.where(low, first, mixed), jnp.where(low, mixed, second)], axis=0
        )

    def block_row(t, b):
        return shuffled[pl.ds(pl.multiple_of((t * BLOCKS + b) * 8, 8), 8), :]

    def permute(k):
        def part(r, carry):
            lo = k * CHUNK_ROWS + r * SUB
            for n in range(4):
                value = jnp.dot(
                    probes[pl.ds(pl.multiple_of(lo, SUB), SUB), :],
                    shuffle[:, n * 256 : (n + 1) * 256],
                    preferred_element_type=F32,
                )
                for h in range(2):
                    shuffled[pl.ds(lo * 8 + 2 * n + h, SUB, stride=8), :] = value[
                        :, h * 128 : (h + 1) * 128
                    ]
            return carry

        lax.fori_loop(0, CHUNK_ROWS // SUB, part, 0)

    def pick_shared():
        row = lax.broadcasted_iota(jnp.int32, (2 * DAYS, ROWS), 0)
        column = lax.broadcasted_iota(jnp.int32, (2 * DAYS, ROWS), 1)
        second = row >= DAYS
        day = jnp.where(second, row - DAYS, row)
        wanted = day * BLOCKS + jnp.where(second, shared_blocks[0, 1], shared_blocks[0, 0])
        select = jnp.where(column == wanted, 1.0, 0.0).astype(BF16)
        for n in range(4):
            cols = slice(n * 256, (n + 1) * 256)
            picked[:, cols] = jnp.dot(
                select, probes[:, cols], preferred_element_type=F32
            ).astype(BF16)
        for n in range(4):
            value = jnp.dot(
                picked[...], shuffle[:, n * 256 : (n + 1) * 256], preferred_element_type=F32
            )
            for h in range(2):
                picked_shuffled[pl.ds(2 * n + h, 2 * DAYS, stride=8), :] = value[
                    :, h * 128 : (h + 1) * 128
                ]

        def days(g, carry):
            for i in range(4):
                t = g * 4 + i
                tiles = [
                    picked_shuffled[pl.ds(pl.multiple_of((m * DAYS + t) * 8, 8), 8), :]
                    for m in range(2)
                ]
                shared[t // CHUNK_DAYS, me, day_rows(t % CHUNK_DAYS), :] = pair_up(*tiles).astype(BF16)
            return carry

        lax.fori_loop(0, DAYS // 4, days, 0)

    def order(k):
        def days(g, carry):
            for i in range(4):
                t = g * 4 + i
                for pair in range(BLOCKS // 2):
                    value = pair_up(block_row(t, 2 * pair), block_row(t, 2 * pair + 1))
                    total[day_rows(t), pair * 128 : (pair + 1) * 128] = value
                    ordered[day_rows(t), pair * 128 : (pair + 1) * 128] = value.astype(BF16)
            return carry

        lax.fori_loop(k * CHUNK_DAYS // 4, (k + 1) * CHUNK_DAYS // 4, days, 0)

    used = [0]
    pending = []

    def send(slot, k, lo, rows, to):
        i = used[0]
        used[0] += 1
        where = shared.at[k, slot, pl.ds(lo, rows)]
        copy = pltpu.make_async_remote_copy(
            src_ref=where,
            dst_ref=where,
            send_sem=send_sem.at[i],
            recv_sem=recv_sem.at[i],
            device_id=(tm, to),
            device_id_type=MESH,
        )
        copy.start()
        pending.append(copy)
        return copy

    flows = [{} for _ in range(CHUNKS)]
    across = {"near": [], "middle": [], "last": []}
    N = CHUNK_ROWS

    def send_own(k):
        f = flows[k]
        f["y"] = send(me, k, 0, N, at(0, 1, 0))
        f["p0"] = send(me, k, 0, N, at(1, 0, 0))
        f["m0"] = send(me, k, 0, N, at(3, 0, 0))
        across["near"].append(send(me, k, 0, N, sibling))

    def relay_first(k):
        f = flows[k]
        f["y"].wait_recv()
        f["p1"] = send(at(0, 1, 0), k, 0, HALF, at(1, 0, 0))
        f["m1"] = send(at(0, 1, 0), k, HALF, HALF, at(3, 0, 0))
        across["near"].append(send(at(0, 1, 0), k, 0, N, sibling))

    def relay_own_row(k):
        f = flows[k]
        f["p0"].wait_recv()
        f["pp0"] = send(at(3, 0, 0), k, 0, HALF, at(1, 0, 0))
        f["yp"] = send(at(3, 0, 0), k, HALF, HALF, at(0, 1, 0))
        across["near"].append(send(at(3, 0, 0), k, 0, N, sibling))
        f["m0"].wait_recv()
        f["mm0"] = send(at(1, 0, 0), k, HALF, HALF, at(3, 0, 0))
        f["ym"] = send(at(1, 0, 0), k, 0, HALF, at(0, 1, 0))
        across["near"].append(send(at(1, 0, 0), k, 0, N, sibling))

    def relay_second(k):
        f = flows[k]
        f["p1"].wait_recv()
        f["pp1"] = send(at(3, 1, 0), k, 0, HALF, at(1, 0, 0))
        f["m1"].wait_recv()
        f["mm1"] = send(at(1, 1, 0), k, HALF, HALF, at(3, 0, 0))

    def relay_third(k):
        f = flows[k]
        f["pp0"].wait_recv()
        f["mm0"].wait_recv()
        across["middle"].append(send(at(2, 0, 0), k, 0, N, sibling))
        f["yp"].wait_recv()
        across["middle"].append(send(at(3, 1, 0), k, 0, N, sibling))
        f["ym"].wait_recv()
        across["middle"].append(send(at(1, 1, 0), k, 0, N, sibling))

    def relay_fourth(k):
        f = flows[k]
        f["pp1"].wait_recv()
        f["mm1"].wait_recv()
        across["last"].append(send(at(2, 1, 0), k, 0, N, sibling))

    def all_here(stage):
        for copy in across[stage]:
            copy.wait_recv()

    def turn(weight, degree, first):
        for pair in range(BLOCKS // 2):
            for n in range(degree):
                tiles[pair, first + n] = jnp.transpose(
                    jnp.concatenate(
                        [weight[2 * pair, n].astype(F32), weight[2 * pair + 1, n].astype(F32)], axis=0
                    )
                ).astype(BF16)

    def build(links, count, degree, first, out):
        def pair_of(pair, carry):
            parts = [tiles[pair, first + n] for n in range(degree)]
            wanted = [
                jnp.where(low[0:1], links[n, 2 * pair], links[n, 2 * pair + 1])
                for n in range(degree)
            ]

            def source_blocks(g, c):
                for i in range(4):
                    r = g * 4 + i
                    terms = [
                        p * jnp.where(w == r, 1.0, 0.0).astype(BF16) for p, w in zip(parts, wanted)
                    ]
                    out[
                        pl.ds(pl.multiple_of(r * BS, BS), BS),
                        pl.ds(pl.multiple_of(pair * 128, 128), 128),
                    ] = functools.reduce(lambda u, v: u + v, terms)
                return c

            return lax.fori_loop(0, count // 4, source_blocks, carry)

        lax.fori_loop(0, BLOCKS // 2, pair_of, 0)

    def build_inverse():
        forth[...] = jnp.zeros_like(forth)
        back[...] = jnp.zeros_like(back)
        gap = jnp.zeros((BS, BS), F32)
        for b in range(BLOCKS):
            quad, place = b // 4, b % 4
            value = inverse_w[b].astype(F32)
            for out, tile in ((forth, jnp.transpose(value)), (back, value)):
                wide = jnp.concatenate([tile, gap] if place % 2 == 0 else [gap, tile], axis=1)
                lane = place // 2 * 128
                out[quad, place * BS : (place + 1) * BS, lane : lane + 128] = wide.astype(BF16)

    def couple_local(k):
        def part(r, carry):
            rows = pl.ds(pl.multiple_of(r * SUB, SUB), SUB)
            for n in range(4):
                cols = slice(n * 256, (n + 1) * 256)
                total[rows, cols] = total[rows, cols] - jnp.dot(
                    ordered[rows, :], near[:, cols], preferred_element_type=F32
                )
            return carry

        lax.fori_loop(k * (CHUNK_ROWS // SUB), (k + 1) * (CHUNK_ROWS // SUB), part, 0)

    def couple_remote(*chips, rows_of=range(CHUNKS)):
        places = [at(dx, dy, 0) // 2 for dx, dy in chips]

        def part(r, carry):
            rows = pl.ds(pl.multiple_of(r * SUB, SUB), SUB)
            k = r // (CHUNK_ROWS // SUB)
            inner = pl.ds(pl.multiple_of(r % (CHUNK_ROWS // SUB) * SUB, SUB), SUB)
            for n in range(4):
                cols = slice(n * 256, (n + 1) * 256)
                left = jnp.concatenate(
                    [shared[k, 2 * q + c, inner, :] for q in places for c in range(2)], axis=1
                )
                right = jnp.concatenate(
                    [far[pl.ds(pl.multiple_of(q * 256, 256), 256), cols] for q in places], axis=0
                )
                total[rows, cols] = total[rows, cols] - jnp.dot(
                    left, right, preferred_element_type=F32
                )
            return carry

        steps = CHUNK_ROWS // SUB
        lax.fori_loop(rows_of[0] * steps, (rows_of[-1] + 1) * steps, part, 0)

    def force(k):
        def part(r, carry):
            rows = pl.ds(pl.multiple_of(r * SUB, SUB), SUB)
            for n in range(4):
                cols = slice(n * 256, (n + 1) * 256)
                states[rows, cols] = jnp.dot(
                    total[rows, cols].astype(BF16), forth[n], preferred_element_type=F32
                )
            return carry

        lax.fori_loop(k * (CHUNK_ROWS // SUB), (k + 1) * (CHUNK_ROWS // SUB), part, 0)

    def scan_forward(k, state):
        def day(t, s):
            s = s * retain[pl.ds(t, 1), :] + states[day_rows(t), :] * active[pl.ds(t, 1), :]
            states[day_rows(t), :] = s
            return s

        return lax.fori_loop(k * CHUNK_DAYS, (k + 1) * CHUNK_DAYS, day, state)

    def prepare_decay():
        on = lax.broadcasted_iota(jnp.int32, (DAYS, WIDTH), 0) < slab_days[0]
        active[...] = jnp.where(on, 1.0, 0.0)
        retain[0:DAYS, :] = jnp.where(on, retention_ref[...], 1.0)
        retain[DAYS : DAYS + 8, :] = jnp.ones((8, WIDTH), F32)

        def ahead(t, d):
            d = d * retain[pl.ds(t, 1), :]
            forward_decay[pl.ds(t, 1), :] = d
            return d

        product = lax.fori_loop(0, DAYS, ahead, jnp.ones((1, WIDTH), F32))

        def behind(i, d):
            t = DAYS - 1 - i
            d = d * retain[pl.ds(t + 1, 1), :]
            backward_decay[pl.ds(t, 1), :] = d
            return d

        lax.fori_loop(0, DAYS, behind, jnp.ones((1, WIDTH), F32))
        for q in range(8):
            slab_decay[tm, q : q + 1, :] = product[:, q * 128 : (q + 1) * 128]

    def tm_copy(buf, to, send, recv):
        return pltpu.make_async_remote_copy(
            src_ref=buf.at[tm],
            dst_ref=buf.at[tm],
            send_sem=tm_send.at[send],
            recv_sem=tm_recv.at[recv],
            device_id=(to, space),
            device_id_type=MESH,
        )

    def exchange(kind, buf, act):
        for d in reversed(range(1, SLABS)):
            ahead = (kind == 1) == (act != "wait_recv")
            other = tm + d if ahead else tm - d
            real = other < SLABS if ahead else other >= 0
            peer = (other + SLABS) % SLABS
            signal = peer if act == "wait_recv" else tm

            @pl.when(real)
            def _():
                getattr(tm_copy(buf, peer, peer, signal), act)()

    def prepare_response():
        for n in range(4):
            cols = slice(n * 256, (n + 1) * 256)
            decay = forward_decay[:, cols]
            gram = lax.dot_general(
                decay * active[:, cols],
                decay,
                (((0,), (0,)), ((), ())),
                precision=lax.Precision.HIGHEST,
                preferred_element_type=F32,
            )
            response[n] = gram * back[n].astype(F32)

    def decay_of(s):
        return jnp.concatenate([slab_decay[s, q : q + 1, :] for q in range(8)], axis=1)

    for k in range(CHUNKS):
        fetch[k].wait()
    pick_shared()
    for copy in weights:
        copy.start()
    pl.semaphore_wait(barrier, 4 + SLABS - 1)
    for k in range(CHUNKS):
        send_own(k)
    prepare_decay()
    decay_copies = [
        tm_copy(slab_decay, (tm + d) % SLABS, SLABS + d - 1, SLABS + d - 1)
        for d in range(1, SLABS)
    ]
    for copy in decay_copies:
        copy.start()
    permute(0)
    permute(1)
    order(0)
    order(1)
    weights[0].wait()
    weights[1].wait()
    turn(local_w, 4, 0)
    turn(remote_w, 2, 4)
    weights[2].wait()
    build_inverse()
    prepare_response()
    relay_first(0)
    relay_own_row(0)
    relay_first(1)
    relay_own_row(1)
    build(local_links, BLOCKS, 4, 0, near)
    build(remote_links, 2 * GROUPS, 2, 4, far)
    couple_local(0)
    relay_second(0)
    couple_local(1)
    relay_second(1)
    all_here("near")
    couple_remote((0, 0), (1, 0), (3, 0), (0, 1))
    relay_third(0)
    relay_third(1)
    all_here("middle")
    couple_remote((2, 0), (1, 1), (3, 1))
    relay_fourth(0)
    relay_fourth(1)
    state = jnp.zeros((PROBES, WIDTH), F32)
    for k in range(CHUNKS):
        across["last"][k].wait_recv()
        couple_remote((2, 1), rows_of=[k])
        force(k)
        state = scan_forward(k, state)
    ends[tm] = state.astype(BF16)
    exchange(1, ends, "start")

    row8 = lax.broadcasted_iota(jnp.int32, (8, 128), 0)

    def fold(values):
        for step in (1, 2, 4):
            keep = (row8 & step) == 0
            values = [
                jnp.where(keep, u, v) + pltpu.roll(jnp.where(keep, v, u), step, 0)
                for u, v in zip(values[0::2], values[1::2])
            ]
        return values[0]

    def adjoint_sweep(carry, with_sums):
        def fix(g, c):
            for i in range(2):
                t = 2 * g + i
                value = states[day_rows(t), :]
                if with_sums:
                    value = value + forward_decay[pl.ds(t, 1), :] * c
                stored[day_rows(t), :] = value.astype(BF16)
            return c

        lax.fori_loop(0, DAYS // 2, fix, carry)

        def part(r, c):
            rows = pl.ds(pl.multiple_of(r * SUB, SUB), SUB)
            for n in range(4):
                cols = slice(n * 256, (n + 1) * 256)
                total[rows, cols] = jnp.dot(stored[rows, cols], back[n], preferred_element_type=F32)
            return c

        lax.fori_loop(0, ROWS // SUB, part, 0)
        leave = []
        for n in range(4):
            cols = slice(n * 256, (n + 1) * 256)

            def days(i, u):
                g = DAYS // 8 - 1 - i
                sums = [[None] * 8, [None] * 8]
                for j in reversed(range(8)):
                    t = g * 8 + j
                    u = total[day_rows(t), cols] * active[pl.ds(t, 1), cols] + retain[
                        pl.ds(t + 1, 1), cols
                    ] * u
                    if with_sums:
                        product = ordered[day_rows(t), cols].astype(F32) * u
                        for h in range(2):
                            half = product[:, h * 128 : (h + 1) * 128]
                            sums[h][j] = half[0:8] + half[8:16]
                if with_sums:
                    eight = pl.ds(pl.multiple_of(g * 8, 8), 8)
                    for h in range(2):
                        lane = n * 256 + h * 128
                        partial[eight, lane : lane + 128] = fold(sums[h])
                return u

            leave.append(
                lax.fori_loop(0, DAYS // 8, days, jnp.zeros((PROBES, 256), F32))
                * retain[0:1, cols]
            )
        return leave

    leave = adjoint_sweep(0, False)
    for copy in decay_copies:
        copy.wait_recv()
    exchange(1, ends, "wait_recv")
    carry = jnp.zeros((PROBES, WIDTH), F32)
    for s in range(SLABS - 1):
        carry = jnp.where(s < tm, decay_of(s) * carry + ends[s].astype(F32), carry)
    for n in range(4):
        cols = slice(n * 256, (n + 1) * 256)
        value = leave[n] + jnp.dot(
            carry[:, cols],
            response[n],
            precision=lax.Precision.HIGHEST,
            preferred_element_type=F32,
        )
        leaving[tm, :, cols] = value.astype(BF16)
    exchange(2, leaving, "start")
    adjoint_sweep(carry, True)

    for copy in pending:
        copy.wait_send()
    for copy in decay_copies:
        copy.wait_send()
    exchange(1, ends, "wait_send")
    exchange(2, leaving, "wait_recv")

    carry = jnp.zeros((PROBES, WIDTH), F32)
    for s in reversed(range(1, SLABS)):
        carry = jnp.where(s > tm, decay_of(s) * carry + leaving[s].astype(F32), carry)

    def finish(g, c):
        eight = pl.ds(pl.multiple_of(g * 8, 8), 8)
        for n in range(8):
            cols = slice(n * 128, (n + 1) * 128)
            top, bottom = c[0:8, cols], c[8:16, cols]
            z = ordered[pl.ds(pl.multiple_of(g * 128, 128), 128), cols].astype(F32)
            extra = fold(
                [
                    z[16 * d : 16 * d + 8] * top + z[16 * d + 8 : 16 * d + 16] * bottom
                    for d in range(8)
                ]
            )
            out_ref[eight, cols] = (partial[eight, cols] + backward_decay[eight, cols] * extra) * (
                1.0 / PROBES
            )
        return c

    lax.fori_loop(0, DAYS // 8, finish, carry)
    exchange(2, leaving, "wait_send")


def local(
    probes,
    local_links,
    remote_links,
    shared_blocks,
    slab_days,
    local_coupling,
    remote_coupling,
    block_inverse,
    retention,
):
    smem = pl.BlockSpec(memory_space=pltpu.SMEM)
    vmem = pl.BlockSpec(memory_space=pltpu.VMEM)
    anywhere = pl.BlockSpec(memory_space=pl.ANY)
    return pl.pallas_call(
        kernel,
        out_shape=jax.ShapeDtypeStruct((DAYS, WIDTH), F32),
        in_specs=[smem] * 4 + [anywhere] * 4 + [vmem],
        out_specs=vmem,
        scratch_shapes=[
            pltpu.VMEM((ROWS, WIDTH), BF16),
            pltpu.VMEM(local_coupling.shape, BF16),
            pltpu.VMEM(remote_coupling.shape, BF16),
            pltpu.VMEM(block_inverse.shape, BF16),
            pltpu.VMEM((WIDTH, WIDTH), BF16),
            pltpu.VMEM((ROWS * 8, 128), F32),
            pltpu.VMEM((2 * DAYS, WIDTH), BF16),
            pltpu.VMEM((2 * DAYS * 8, 128), F32),
            pltpu.VMEM((ROWS, WIDTH), BF16),
            pltpu.VMEM((CHUNKS, GROUPS, CHUNK_ROWS, 128), BF16),
            pltpu.VMEM((BLOCKS // 2, 6, BS, 128), BF16),
            pltpu.VMEM((WIDTH, WIDTH), BF16),
            pltpu.VMEM((2 * WIDTH, WIDTH), BF16),
            pltpu.VMEM((4, 256, 256), BF16),
            pltpu.VMEM((4, 256, 256), BF16),
            pltpu.VMEM((ROWS, WIDTH), F32),
            pltpu.VMEM((ROWS, WIDTH), F32),
            pltpu.VMEM((ROWS, WIDTH), BF16),
            pltpu.VMEM((DAYS + 8, WIDTH), F32),
            pltpu.VMEM((DAYS, WIDTH), F32),
            pltpu.VMEM((DAYS, WIDTH), F32),
            pltpu.VMEM((DAYS, WIDTH), F32),
            pltpu.VMEM((DAYS, WIDTH), F32),
            pltpu.VMEM((SLABS, 8, 128), F32),
            pltpu.VMEM((4, 256, 256), F32),
            pltpu.VMEM((SLABS, PROBES, WIDTH), BF16),
            pltpu.VMEM((SLABS, PROBES, WIDTH), BF16),
            pltpu.SemaphoreType.DMA((CHUNKS + 3,)),
            pltpu.SemaphoreType.DMA((CHUNKS * 19,)),
            pltpu.SemaphoreType.DMA((CHUNKS * 19,)),
            pltpu.SemaphoreType.DMA((2 * SLABS - 1,)),
            pltpu.SemaphoreType.DMA((2 * SLABS - 1,)),
        ],
        compiler_params=pltpu.CompilerParams(
            vmem_limit_bytes=60 << 20, collective_id=0, has_side_effects=True
        ),
    )(
        local_links.T,
        remote_links.T,
        shared_blocks,
        slab_days,
        probes.reshape(ROWS, WIDTH),
        local_coupling,
        remote_coupling,
        block_inverse,
        retention,
    )


def solution(mesh):
    placed = (
        P("tm", "space", None),
        P("space", None),
        P("space", None),
        P("space", None),
        P("tm"),
        P("space", None, None, None),
        P("space", None, None, None),
        P("space", None, None),
        P("tm", "space"),
    )
    return jax.shard_map(
        local, mesh=mesh, in_specs=placed, out_specs=P("tm", "space"), check_vma=False
    )
```
